32 devices in a mesh: gx: 2 (over x), gy: 4 (over z), gz: 4 (over y, core).
Axes of the slice: x: 2, y: 2, z: 4, core: 2. Of those that a mesh axis runs over, the one named last changes fastest.
Arguments:
- species_field: float32 [256, 128, 512], P('gx', 'gy', 'gz'), may hold values from -40 to 40
- test_matrix: float32 [48, 128, 512], P(None, 'gy', 'gz'), may hold values from -0.0234375 to 0.0234375
Outputs:
- core_tensor: float32 [48, 128, 512], P('gx', 'gy', 'gz')
The draws below stay inside these ranges and needn't reach their ends.
All inputs are finite; a program needn't handle non-finite values.
Results may differ from the reference program's by a relative error of at most 0.000075.
Values sent between devices are 32-bit elements; how exact they have to be, the bound alone decides.
No kernel may reach another device: no remote copies, remote signals or barrier semaphores. Data moves between devices by JAX's collectives and lax.ppermute only.
A program may use at most 64 MiB of HBM per device.

```python
import math
import jax
import jax.numpy as jnp
from jax import lax

R = 48
NX = 256
NY = 128
NZ = 512


def scaled_field(key, spread, base_values):
    key_rows, key_columns = jax.random.split(key, 2)
    position = jnp.arange(NX, dtype=jnp.float32) / max(NX - 1, 1)
    row_scale = jnp.exp(math.log(3.0) * (position - 0.5) + jax.random.uniform(key_rows, (NX,), jnp.float32, -spread, spread))
    column_scale = jnp.exp(jax.random.uniform(key_columns, (NY,), jnp.float32, -spread, spread))
    return base_values * row_scale[:, None, None] * column_scale[None, :, None]


def draw_species_field(key, part):
    key = jax.random.fold_in(key, 11)
    key_values, key_scales = jax.random.split(key, 2)
    base_values = jnp.clip(jax.random.normal(key_values, (NX, NY, NZ), jnp.float32), -6.0, 6.0)
    return scaled_field(key_scales, 0.6, base_values)


def block_scale(key, dims, cuts, least, top_value):
    def one(dim, blocks):
        steps = jax.random.uniform(jax.random.fold_in(jax.random.fold_in(key, 6), dim), (blocks,), jnp.float32, least / len(cuts), top_value / len(cuts))
        return jnp.repeat(jnp.exp(steps), dims[dim] // blocks).reshape((-1,) + (1,) * (len(dims) - dim - 1))

    gain = one(*cuts[0])
    for cut in cuts[1:]:
        gain = gain * one(*cut)
    return gain


def scatter_about(own_key, dims, scale, reach, cuts=(), kind=jnp.bfloat16):
    array = jax.random.normal(own_key, dims, jnp.float32) * scale
    if len(cuts) > 0:
        array = block_scale(own_key, dims, cuts, -0.22, 0.18) * array
    return jnp.clip(array, min=-reach, max=reach).astype(kind)


def setup_inputs(seed: int = 0) -> dict:
    arg_keys = jax.random.split(jax.random.key(seed), 3)
    return {
        "species_field": draw_species_field(jax.random.fold_in(arg_keys[2], 71), 0),
        "test_matrix": scatter_about(arg_keys[1], (R, NY, NZ), (NY * NZ) ** -0.5, 0.0234375, ((1, 4), (2, 4)), jnp.float32),
    }


PRECISE = lax.Precision.HIGHEST

def reference(species_field, test_matrix):
    sketch = jnp.einsum('ijk,rjk->ir', species_field, test_matrix, precision=PRECISE)
    gram_matrix = jnp.dot(sketch.T, sketch, precision=PRECISE)
    cholesky_factor = jnp.linalg.cholesky(gram_matrix)
    factor_t = lax.linalg.triangular_solve(cholesky_factor, sketch.T, left_side=True, lower=True)
    core_tensor = jnp.einsum('ri,ijk->rjk', factor_t, species_field, precision=PRECISE)
    return core_tensor
```

```python
import functools

import jax
import jax.numpy as jnp
from jax import lax
from jax.experimental import pallas as pl
from jax.experimental.pallas import tpu as pltpu
from jax.sharding import PartitionSpec as P

F32, BF16 = jnp.float32, jnp.bfloat16
PRECISE = lax.Precision.HIGHEST
NT = (((1,), (1,)), ((), ()))
NN = (((1,), (0,)), ((), ()))
LANES, SUBLANES = 128, 8
VMEM_LIMIT = 48 << 20


def split(x, parts):
    terms = []
    for _ in range(parts - 1):
        terms.append(x.astype(BF16))
        x = x - terms[-1].astype(F32)
    return terms + [x.astype(BF16)]


def sketch_kernel(span, field_hbm, test_hbm, sketch_ref, pairs_ref, field, test, sems):
    rows, second, lanes = field_hbm.shape
    columns = test_hbm.shape[0]
    steps = second // span
    copies = []
    for step in range(steps):
        part = pl.ds(step * span, span)
        for which, (source, target) in enumerate(((field_hbm, field), (test_hbm, test))):
            copy = pltpu.make_async_copy(source.at[:, part], target.at[step], sems.at[which, step])
            copy.start()
            copies.append(copy)
    total = low = None
    for step in range(steps):
        copies[2 * step].wait()
        copies[2 * step + 1].wait()
        flat_field = field.at[step].reshape(rows * span, lanes)
        flat_test = test.at[step].reshape(columns * span, lanes)
        for pair in range(span // 2):
            x = jnp.concatenate([flat_field[pl.ds(2 * pair + q, rows, stride=span), :] for q in range(2)], axis=1)
            t = jnp.concatenate([flat_test[pl.ds(2 * pair + q, columns, stride=span), :] for q in range(2)], axis=1)
            x = split(x, 3)
            t = split(t, 3)
            weights = jnp.concatenate(x[:2], axis=0)
            pairs_ref[step * span // 2 + pair] = weights
            term = lax.dot_general(jnp.concatenate(t, axis=0), weights, NT, preferred_element_type=F32)
            rest = lax.dot_general(t[0], x[2], NT, preferred_element_type=F32)
            total = term if total is None else total + term
            low = rest if low is None else low + rest
    for part in reversed(range(3)):
        block = total[part * columns : (part + 1) * columns]
        low = low + block[:, rows:] + block[:, :rows] if part else (low + block[:, rows:]) + block[:, :rows]
    sketch_ref[...] = low


def partial_sketch(field, test):
    rows, second, lanes = field.shape
    columns = test.shape[0]
    span = SUBLANES
    steps = second // span
    return pl.pallas_call(
        functools.partial(sketch_kernel, span),
        in_specs=[pl.BlockSpec(memory_space=pl.ANY)] * 2,
        out_shape=[
            jax.ShapeDtypeStruct((columns, rows), F32),
            jax.ShapeDtypeStruct((second // 2, 2 * rows, 2 * lanes), BF16),
        ],
        scratch_shapes=[
            pltpu.VMEM((steps, rows, span, lanes), F32),
            pltpu.VMEM((steps, columns, span, lanes), F32),
            pltpu.SemaphoreType.DMA((2, steps)),
        ],
        compiler_params=pltpu.CompilerParams(vmem_limit_bytes=VMEM_LIMIT),
        name="partial_sketch",
    )(field, test)


def eliminate(gram, right):
    size = gram.shape[0]
    whole = jnp.concatenate([jnp.pad(gram, ((0, 0), (0, LANES - size))), right], axis=1)
    tiles = [whole[i : i + SUBLANES] for i in range(0, size, SUBLANES)]
    row_ids = lax.broadcasted_iota(jnp.int32, (SUBLANES, 1), 0)
    solved = []
    for k in range(size):
        first, at = divmod(k, SUBLANES)
        row = tiles[first][at : at + 1]
        pivot = row[:, k : k + 1]
        scaled = row * (1.0 / pivot)
        solved.append(row[:, LANES:] * lax.rsqrt(pivot))
        for i in range(first, len(tiles)):
            column = tiles[i][:, k : k + 1]
            if i == first:
                column = jnp.where(row_ids > at, column, 0.0)
            tiles[i] = tiles[i] - column * scaled
    return jnp.concatenate(solved, axis=0)


def project_kernel(axis, sketch_ref, pairs_ref, *out_refs):
    pairs, rows, lanes = pairs_ref.shape[0], pairs_ref.shape[1] // 2, pairs_ref.shape[2] // 2
    sketch = sketch_ref[...]
    gram = lax.dot_general(sketch, sketch, NT, precision=PRECISE, preferred_element_type=F32)
    factor = eliminate(gram, sketch[:, :rows])
    parties = len(out_refs)
    ranks = factor.shape[0] // parties
    me = lax.axis_index(axis)
    ordered = []
    for d in range(parties):
        rank_rows = factor[:ranks]
        for e in range(1, parties):
            rank_rows = jnp.where((me ^ d) == e, factor[e * ranks : (e + 1) * ranks], rank_rows)
        ordered.append(rank_rows)
    factor = jnp.concatenate(ordered, axis=0)
    high, low = split(factor, 2)
    left = jnp.concatenate([jnp.concatenate([high, high], axis=1), jnp.concatenate([low, low], axis=1)], axis=0)
    flat = [ref.reshape(ranks * 2 * pairs, lanes) for ref in out_refs]
    for pair in range(pairs):
        product = lax.dot_general(left, pairs_ref[pair], NN, preferred_element_type=F32)
        product = product[: factor.shape[0]] + product[factor.shape[0] :]
        for q in range(2):
            for d in range(parties):
                flat[d][pl.ds(2 * pair + q, ranks, stride=2 * pairs), :] = product[
                    d * ranks : (d + 1) * ranks, q * lanes : (q + 1) * lanes
                ]


def project(sketch, pairs, axis, parties):
    columns = sketch.shape[0]
    out = jax.ShapeDtypeStruct((columns // parties, 2 * pairs.shape[0], pairs.shape[2] // 2), F32)
    return pl.pallas_call(
        functools.partial(project_kernel, axis),
        out_shape=[out] * parties,
        compiler_params=pltpu.CompilerParams(vmem_limit_bytes=VMEM_LIMIT),
        name="project",
    )(sketch, pairs)


def exchange(x, axis, size, bit):
    return lax.ppermute(x, axis, [(i, i ^ bit) for i in range(size)])


def bits(size):
    return [1 << b for b in range(size.bit_length() - 1)]


def body(sizes, field, test):
    sketch, pairs = partial_sketch(field, test)
    for axis in ("gz", "gy"):
        for bit in bits(sizes[axis]):
            sketch = sketch + exchange(sketch, axis, sizes[axis], bit)
    for bit in bits(sizes["gx"]):
        sketch = jnp.concatenate([sketch, exchange(sketch, "gx", sizes["gx"], bit)], axis=1)
    products = project(sketch, pairs, "gx", sizes["gx"])
    core = products[0]
    for d in range(1, sizes["gx"]):
        core = core + exchange(products[d], "gx", sizes["gx"], d)
    return core


def solution(mesh):
    in_specs = (P("gx", "gy", "gz"), P(None, "gy", "gz"))
    out_specs = P("gx", "gy", "gz")
    step = functools.partial(body, dict(mesh.shape))
    return jax.shard_map(step, mesh=mesh, in_specs=in_specs, out_specs=out_specs, check_vma=False)
```

```python
import functools

import jax
import jax.numpy as jnp
from jax import lax
from jax.experimental import pallas as pl
from jax.experimental.pallas import tpu as pltpu
from jax.sharding import PartitionSpec as P

F32, BF16 = jnp.float32, jnp.bfloat16
PRECISE = lax.Precision.HIGHEST
NT = (((1,), (1,)), ((), ()))
NN = (((1,), (0,)), ((), ()))
LANES, SUBLANES = 128, 8
VMEM_LIMIT = 48 << 20


def split(x, parts):
    terms = []
    for _ in range(parts - 1):
        terms.append(x.astype(BF16))
        x = x - terms[-1].astype(F32)
    return terms + [x.astype(BF16)]


def sketch_kernel(span, field_hbm, test_hbm, sketch_ref, pairs_ref, field, test, sems):
    rows, second, lanes = field_hbm.shape
    columns = test_hbm.shape[0]
    steps = second // span
    copies = []
    for step in range(steps):
        part = pl.ds(step * span, span)
        for which, (source, target) in enumerate(((field_hbm, field), (test_hbm, test))):
            copy = pltpu.make_async_copy(source.at[:, part], target.at[step], sems.at[which, step])
            copy.start()
            copies.append(copy)
    total = low = None
    for step in range(steps):
        copies[2 * step].wait()
        copies[2 * step + 1].wait()
        flat_field = field.at[step].reshape(rows * span, lanes)
        flat_test = test.at[step].reshape(columns * span, lanes)
        for pair in range(span // 2):
            x = jnp.concatenate([flat_field[pl.ds(2 * pair + q, rows, stride=span), :] for q in range(2)], axis=1)
            t = jnp.concatenate([flat_test[pl.ds(2 * pair + q, columns, stride=span), :] for q in range(2)], axis=1)
            x = split(x, 3)
            t = split(t, 3)
            weights = jnp.concatenate(x[:2], axis=0)
            pairs_ref[step * span // 2 + pair] = weights
            term = lax.dot_general(jnp.concatenate(t, axis=0), weights, NT, preferred_element_type=F32)
            rest = lax.dot_general(t[0], x[2], NT, preferred_element_type=F32)
            total = term if total is None else total + term
            low = rest if low is None else low + rest
    for part in reversed(range(3)):
        block = total[part * columns : (part + 1) * columns]
        low = low + block[:, rows:] + block[:, :rows] if part else (low + block[:, rows:]) + block[:, :rows]
    sketch_ref[...] = low


def partial_sketch(field, test):
    rows, second, lanes = field.shape
    columns = test.shape[0]
    span = SUBLANES
    steps = second // span
    return pl.pallas_call(
        functools.partial(sketch_kernel, span),
        in_specs=[pl.BlockSpec(memory_space=pl.ANY)] * 2,
        out_shape=[
            jax.ShapeDtypeStruct((columns, rows), F32),
            jax.ShapeDtypeStruct((second // 2, 2 * rows, 2 * lanes), BF16),
        ],
        scratch_shapes=[
            pltpu.VMEM((steps, rows, span, lanes), F32),
            pltpu.VMEM((steps, columns, span, lanes), F32),
            pltpu.SemaphoreType.DMA((2, steps)),
        ],
        compiler_params=pltpu.CompilerParams(vmem_limit_bytes=VMEM_LIMIT),
        name="partial_sketch",
    )(*(pltpu.with_memory_space_constraint(array, pltpu.HBM) for array in (field, test)))


def eliminate(gram, right):
    size = gram.shape[0]
    whole = jnp.concatenate([jnp.pad(gram, ((0, 0), (0, LANES - size))), right], axis=1)
    tiles = [whole[i : i + SUBLANES] for i in range(0, size, SUBLANES)]
    row_ids = lax.broadcasted_iota(jnp.int32, (SUBLANES, 1), 0)
    solved = []
    for k in range(size):
        first, at = divmod(k, SUBLANES)
        row = tiles[first][at : at + 1]
        pivot = row[:, k : k + 1]
        scaled = row * (1.0 / pivot)
        solved.append(row[:, LANES:] * lax.rsqrt(pivot))
        for i in range(first, len(tiles)):
            column = tiles[i][:, k : k + 1]
            if i == first:
                column = jnp.where(row_ids > at, column, 0.0)
            tiles[i] = tiles[i] - column * scaled
    return jnp.concatenate(solved, axis=0)


def project_kernel(axis, sketch_ref, pairs_ref, *out_refs):
    pairs, rows, lanes = pairs_ref.shape[0], pairs_ref.shape[1] // 2, pairs_ref.shape[2] // 2
    sketch = sketch_ref[...]
    gram = lax.dot_general(sketch, sketch, NT, precision=PRECISE, preferred_element_type=F32)
    factor = eliminate(gram, sketch[:, :rows])
    parties = len(out_refs)
    ranks = factor.shape[0] // parties
    me = lax.axis_index(axis)
    ordered = []
    for d in range(parties):
        rank_rows = factor[:ranks]
        for e in range(1, parties):
            rank_rows = jnp.where((me ^ d) == e, factor[e * ranks : (e + 1) * ranks], rank_rows)
        ordered.append(rank_rows)
    factor = jnp.concatenate(ordered, axis=0)
    high, low = split(factor, 2)
    left = jnp.concatenate([jnp.concatenate([high, high], axis=1), jnp.concatenate([low, low], axis=1)], axis=0)
    flat = [ref.reshape(ranks * 2 * pairs, lanes) for ref in out_refs]
    for pair in range(pairs):
        product = lax.dot_general(left, pairs_ref[pair], NN, preferred_element_type=F32)
        product = product[: factor.shape[0]] + product[factor.shape[0] :]
        for q in range(2):
            for d in range(parties):
                flat[d][pl.ds(2 * pair + q, ranks, stride=2 * pairs), :] = product[
                    d * ranks : (d + 1) * ranks, q * lanes : (q + 1) * lanes
                ]


def project(sketch, pairs, axis, parties):
    columns = sketch.shape[0]
    out = jax.ShapeDtypeStruct((columns // parties, 2 * pairs.shape[0], pairs.shape[2] // 2), F32)
    return pl.pallas_call(
        functools.partial(project_kernel, axis),
        out_shape=[out] * parties,
        compiler_params=pltpu.CompilerParams(vmem_limit_bytes=VMEM_LIMIT),
        name="project",
    )(sketch, pairs)


def exchange(x, axis, size, bit):
    return lax.ppermute(x, axis, [(i, i ^ bit) for i in range(size)])


def bits(size):
    return [1 << b for b in range(size.bit_length() - 1)]


def body(sizes, field, test):
    sketch, pairs = partial_sketch(field, test)
    for axis in ("gz", "gy"):
        for bit in bits(sizes[axis]):
            sketch = sketch + exchange(sketch, axis, sizes[axis], bit)
    for bit in bits(sizes["gx"]):
        sketch = jnp.concatenate([sketch, exchange(sketch, "gx", sizes["gx"], bit)], axis=1)
    products = project(sketch, pairs, "gx", sizes["gx"])
    core = products[0]
    for d in range(1, sizes["gx"]):
        core = core + exchange(products[d], "gx", sizes["gx"], d)
    return core


def solution(mesh):
    in_specs = (P("gx", "gy", "gz"), P(None, "gy", "gz"))
    out_specs = P("gx", "gy", "gz")
    step = functools.partial(body, dict(mesh.shape))
    return jax.shard_map(step, mesh=mesh, in_specs=in_specs, out_specs=out_specs, check_vma=False)
```

```python
import functools

import jax
import jax.numpy as jnp
from jax import lax
from jax.experimental import pallas as pl
from jax.experimental.pallas import tpu as pltpu
from jax.sharding import PartitionSpec as P

F32, BF16 = jnp.float32, jnp.bfloat16
PRECISE = lax.Precision.HIGHEST
NT = (((1,), (1,)), ((), ()))
NN = (((1,), (0,)), ((), ()))
LANES, SUBLANES = 128, 8
VMEM_LIMIT = 48 << 20


def split(x, parts):
    terms = []
    for _ in range(parts - 1):
        terms.append(x.astype(BF16))
        x = x - terms[-1].astype(F32)
    return terms + [x.astype(BF16)]


def sketch_kernel(span, field_hbm, test_hbm, sketch_ref, pairs_ref, field, test, sems):
    rows, second, lanes = field_hbm.shape
    columns = test_hbm.shape[0]
    steps = second // span
    copies = []
    for step in range(steps):
        part = pl.ds(step * span, span)
        for which, (source, target) in enumerate(((field_hbm, field), (test_hbm, test))):
            copy = pltpu.make_async_copy(source.at[:, part], target.at[step], sems.at[which, step])
            copy.start()
            copies.append(copy)
    total = low = None
    for step in range(steps):
        copies[2 * step].wait()
        copies[2 * step + 1].wait()
        flat_field = field.at[step].reshape(rows * span, lanes)
        flat_test = test.at[step].reshape(columns * span, lanes)
        for pair in range(span // 2):
            x = jnp.concatenate([flat_field[pl.ds(2 * pair + q, rows, stride=span), :] for q in range(2)], axis=1)
            t = jnp.concatenate([flat_test[pl.ds(2 * pair + q, columns, stride=span), :] for q in range(2)], axis=1)
            x = split(x, 3)
            t = split(t, 3)
            weights = jnp.concatenate(x[:2], axis=0)
            pairs_ref[step * span // 2 + pair] = weights
            term = lax.dot_general(jnp.concatenate(t, axis=0), weights, NT, preferred_element_type=F32)
            rest = lax.dot_general(t[0], x[2], NT, preferred_element_type=F32)
            total = term if total is None else total + term
            low = rest if low is None else low + rest
    for part in reversed(range(3)):
        block = total[part * columns : (part + 1) * columns]
        low = low + block[:, rows:] + block[:, :rows] if part else (low + block[:, rows:]) + block[:, :rows]
    sketch_ref[...] = low


def partial_sketch(field, test):
    rows, second, lanes = field.shape
    columns = test.shape[0]
    span = SUBLANES
    steps = second // span
    return pl.pallas_call(
        functools.partial(sketch_kernel, span),
        in_specs=[pl.BlockSpec(memory_space=pl.ANY)] * 2,
        out_shape=[
            jax.ShapeDtypeStruct((columns, rows), F32),
            jax.ShapeDtypeStruct((second // 2, 2 * rows, 2 * lanes), BF16),
        ],
        scratch_shapes=[
            pltpu.VMEM((steps, rows, span, lanes), F32),
            pltpu.VMEM((steps, columns, span, lanes), F32),
            pltpu.SemaphoreType.DMA((2, steps)),
        ],
        compiler_params=pltpu.CompilerParams(vmem_limit_bytes=VMEM_LIMIT),
        name="partial_sketch",
    )(*(pltpu.with_memory_space_constraint(array, pltpu.HBM) for array in (field, test)))


def eliminate(gram, right):
    size, width = gram.shape[0], LANES + right.shape[1]
    whole = jnp.concatenate([jnp.pad(gram, ((0, 0), (0, LANES - size))), right], axis=1)
    tiles = [whole[i : i + SUBLANES] for i in range(0, size, SUBLANES)]
    spread = lambda x: jnp.broadcast_to(x, (SUBLANES, LANES))
    widen = lambda x: jnp.concatenate([x] * (width // LANES), axis=1)
    block = range(SUBLANES)
    solved = []
    for t, tile in enumerate(tiles):
        start = t * SUBLANES
        columns = [spread(tile[:, start + j : start + j + 1]) for j in block]
        entry = {(i, j): spread(columns[j][i : i + 1]) for j in block for i in range(j, SUBLANES)}
        inverse, lower = [], {}
        for j in block:
            inverse.append(1.0 / entry[j, j])
            for i in range(j + 1, SUBLANES):
                lower[i, j] = entry[i, j] * inverse[j]
            for m in range(j + 1, SUBLANES):
                for i in range(m, SUBLANES):
                    entry[i, m] = entry[i, m] - lower[i, j] * entry[m, j]
        lower = {at: widen(x) for at, x in lower.items()}
        reduced = []
        for i in block:
            row = jnp.broadcast_to(tile[i : i + 1], (SUBLANES, width))
            for j in range(i):
                row = row - lower[i, j] * reduced[j]
            reduced.append(row)
            solved.append(row[:1, LANES:] * widen(lax.rsqrt(entry[i, i]))[:1, LANES:])
        if t == len(tiles) - 1:
            break
        scaled = [None] * SUBLANES
        for i in reversed(block):
            row = reduced[i] * widen(inverse[i])
            for j in range(i + 1, SUBLANES):
                row = row - lower[j, i] * scaled[j]
            scaled[i] = row
        for later in range(t + 1, len(tiles)):
            rest = tiles[later]
            for j in block:
                rest = rest - tiles[later][:, start + j : start + j + 1] * scaled[j]
            tiles[later] = rest
    return jnp.concatenate(solved, axis=0)


def multiply(factor, pairs_ref, first, out_refs):
    count = factor.shape[0]
    ranks, span, lanes = out_refs[0].shape
    high, low = (part.astype(F32) for part in split(factor, 2))
    left = jnp.concatenate([high, low], axis=0)
    left = jnp.concatenate([left, left], axis=1).astype(BF16)
    flat = [ref.reshape(ranks * span, lanes) for ref in out_refs]
    for pair in range(span // 2):
        product = lax.dot_general(left, pairs_ref[first + pair], NN, preferred_element_type=F32)
        product = product[:count] + product[count:]
        for q in range(2):
            for d, ref in enumerate(flat):
                ref[pl.ds(2 * pair + q, ranks, stride=span), :] = product[
                    d * ranks : (d + 1) * ranks, q * lanes : (q + 1) * lanes
                ]


def solve_kernel(axis, sketch_ref, pairs_ref, factor_ref, *out_refs):
    rows = pairs_ref.shape[1] // 2
    sketch = sketch_ref[...]
    gram = lax.dot_general(sketch, sketch, NT, precision=PRECISE, preferred_element_type=F32)
    factor = eliminate(gram, sketch[:, :rows])
    parties = len(out_refs) + 1
    ranks = factor.shape[0] // parties
    me = lax.axis_index(axis)
    ordered = []
    for d in range(parties):
        rank_rows = factor[:ranks]
        for e in range(1, parties):
            rank_rows = jnp.where((me ^ d) == e, factor[e * ranks : (e + 1) * ranks], rank_rows)
        ordered.append(rank_rows)
    factor_ref[...] = jnp.concatenate(ordered, axis=0)
    multiply(jnp.concatenate(ordered[1:], axis=0), pairs_ref, 0, out_refs)


def more_kernel(first, begin, factor_ref, pairs_ref, *out_refs):
    ranks = out_refs[0].shape[0]
    multiply(factor_ref[begin : begin + ranks * len(out_refs), :], pairs_ref, first, out_refs)


def add_kernel(own_ref, *refs):
    *others, out_ref = refs
    place = 0
    span = others[0].shape[1]
    parties = len(others) * span // own_ref.shape[1]
    for chunk in range(len(others) // parties):
        part = pl.ds(chunk * span, span)
        total = own_ref[:, part, :]
        for ref in others[chunk * parties : (chunk + 1) * parties]:
            total = total + ref[...]
        out_ref[:, part, :] = total


PARAMS = pltpu.CompilerParams(vmem_limit_bytes=VMEM_LIMIT)


def project(sketch, pairs, axis, parties, chunks):
    columns, rows = sketch.shape[0], pairs.shape[1] // 2
    lanes = pairs.shape[2] // 2
    ranks, second = columns // parties, 2 * pairs.shape[0]
    chunk = jax.ShapeDtypeStruct((ranks, second // chunks, lanes), F32)
    factor, *sent = pl.pallas_call(
        functools.partial(solve_kernel, axis),
        out_shape=[jax.ShapeDtypeStruct((columns, rows), F32)] + [chunk] * (parties - 1),
        compiler_params=PARAMS,
        name="solve",
    )(sketch, pairs)
    received = [exchange(x, axis, parties, d + 1) for d, x in enumerate(sent)]
    for step in range(1, chunks):
        sent = pl.pallas_call(
            functools.partial(more_kernel, step * (second // chunks) // 2, ranks),
            out_shape=[chunk] * (parties - 1),
            compiler_params=PARAMS,
            name="others_ranks",
        )(factor, pairs)
        received += [exchange(x, axis, parties, d + 1) for d, x in enumerate(sent)]
    own = jax.ShapeDtypeStruct((ranks, second, lanes), F32)
    (core,) = pl.pallas_call(
        functools.partial(more_kernel, 0, 0), out_shape=[own], compiler_params=PARAMS, name="own_ranks"
    )(factor, pairs)
    return pl.pallas_call(add_kernel, out_shape=own, compiler_params=PARAMS, name="add_ranks")(core, *received)


def exchange(x, axis, size, bit):
    return lax.ppermute(x, axis, [(i, i ^ bit) for i in range(size)])


def bits(size):
    return [1 << b for b in range(size.bit_length() - 1)]


def body(sizes, field, test):
    sketch, pairs = partial_sketch(field, test)
    for axis in ("gz", "gy"):
        for bit in bits(sizes[axis]):
            sketch = sketch + exchange(sketch, axis, sizes[axis], bit)
    for bit in bits(sizes["gx"]):
        sketch = jnp.concatenate([sketch, exchange(sketch, "gx", sizes["gx"], bit)], axis=1)
    return project(sketch, pairs, "gx", sizes["gx"], 2)


def solution(mesh):
    in_specs = (P("gx", "gy", "gz"), P(None, "gy", "gz"))
    out_specs = P("gx", "gy", "gz")
    step = functools.partial(body, dict(mesh.shape))
    return jax.shard_map(step, mesh=mesh, in_specs=in_specs, out_specs=out_specs, check_vma=False)
```

```python
import functools

import jax
import jax.numpy as jnp
from jax import lax
from jax.experimental import pallas as pl
from jax.experimental.pallas import tpu as pltpu
from jax.sharding import PartitionSpec as P

F32, BF16 = jnp.float32, jnp.bfloat16
PRECISE = lax.Precision.HIGHEST
NT = (((1,), (1,)), ((), ()))
NN = (((1,), (0,)), ((), ()))
LANES, SUBLANES = 128, 8
VMEM_LIMIT = 48 << 20


def split(x, parts):
    terms = []
    for _ in range(parts - 1):
        terms.append(x.astype(BF16))
        x = x - terms[-1].astype(F32)
    return terms + [x.astype(BF16)]


def sketch_kernel(span, field_hbm, test_hbm, sketch_ref, pairs_ref, field, test, sems):
    rows, second, lanes = field_hbm.shape
    columns = test_hbm.shape[0]
    steps = second // span
    copies = []
    for step in range(steps):
        part = pl.ds(step * span, span)
        for which, (source, target) in enumerate(((field_hbm, field), (test_hbm, test))):
            copy = pltpu.make_async_copy(source.at[:, part], target.at[step], sems.at[which, step])
            copy.start()
            copies.append(copy)
    total = low = None
    for step in range(steps):
        copies[2 * step].wait()
        copies[2 * step + 1].wait()
        flat_field = field.at[step].reshape(rows * span, lanes)
        flat_test = test.at[step].reshape(columns * span, lanes)
        for pair in range(span // 2):
            x = jnp.concatenate([flat_field[pl.ds(2 * pair + q, rows, stride=span), :] for q in range(2)], axis=1)
            t = jnp.concatenate([flat_test[pl.ds(2 * pair + q, columns, stride=span), :] for q in range(2)], axis=1)
            x = split(x, 3)
            t = split(t, 3)
            weights = jnp.concatenate(x[:2], axis=0)
            pairs_ref[step * span // 2 + pair] = weights
            term = lax.dot_general(jnp.concatenate(t, axis=0), weights, NT, preferred_element_type=F32)
            rest = lax.dot_general(t[0], x[2], NT, preferred_element_type=F32)
            total = term if total is None else total + term
            low = rest if low is None else low + rest
    for part in reversed(range(3)):
        block = total[part * columns : (part + 1) * columns]
        low = low + block[:, rows:] + block[:, :rows] if part else (low + block[:, rows:]) + block[:, :rows]
    sketch_ref[...] = low


def partial_sketch(field, test):
    rows, second, lanes = field.shape
    columns = test.shape[0]
    span = SUBLANES
    steps = second // span
    return pl.pallas_call(
        functools.partial(sketch_kernel, span),
        in_specs=[pl.BlockSpec(memory_space=pl.ANY)] * 2,
        out_shape=[
            jax.ShapeDtypeStruct((columns, rows), F32),
            jax.ShapeDtypeStruct((second // 2, 2 * rows, 2 * lanes), BF16),
        ],
        scratch_shapes=[
            pltpu.VMEM((steps, rows, span, lanes), F32),
            pltpu.VMEM((steps, columns, span, lanes), F32),
            pltpu.SemaphoreType.DMA((2, steps)),
        ],
        compiler_params=pltpu.CompilerParams(vmem_limit_bytes=VMEM_LIMIT),
        name="partial_sketch",
    )(*(pltpu.with_memory_space_constraint(array, pltpu.HBM) for array in (field, test)))


def eliminate(gram, right):
    size, width = gram.shape[0], LANES + right.shape[1]
    whole = jnp.concatenate([gram, jnp.zeros((size, LANES - size), F32), right], axis=1)
    tiles = [whole[i : i + SUBLANES] for i in range(0, size, SUBLANES)]
    spread = lambda x: jnp.broadcast_to(x, (SUBLANES, LANES))
    widen = lambda x: jnp.concatenate([x] * (width // LANES), axis=1)
    block = range(SUBLANES)
    solved = []
    for t, tile in enumerate(tiles):
        start = t * SUBLANES
        columns = [spread(tile[:, start + j : start + j + 1]) for j in block]
        entry = {(i, j): spread(columns[j][i : i + 1]) for j in block for i in range(j, SUBLANES)}
        inverse, lower = [], {}
        for j in block:
            inverse.append(1.0 / entry[j, j])
            for i in range(j + 1, SUBLANES):
                lower[i, j] = entry[i, j] * inverse[j]
            for m in range(j + 1, SUBLANES):
                for i in range(m, SUBLANES):
                    entry[i, m] = entry[i, m] - lower[i, j] * entry[m, j]
        lower = {at: widen(x) for at, x in lower.items()}
        reduced = []
        for i in block:
            row = jnp.broadcast_to(tile[i : i + 1], (SUBLANES, width))
            for j in range(i):
                row = row - lower[i, j] * reduced[j]
            reduced.append(row)
            solved.append(row[:1, LANES:] * widen(lax.rsqrt(entry[i, i]))[:1, LANES:])
        if t == len(tiles) - 1:
            break
        scaled = [None] * SUBLANES
        for i in reversed(block):
            row = reduced[i] * widen(inverse[i])
            for j in range(i + 1, SUBLANES):
                row = row - lower[j, i] * scaled[j]
            scaled[i] = row
        for later in range(t + 1, len(tiles)):
            rest = tiles[later]
            for j in block:
                rest = rest - tiles[later][:, start + j : start + j + 1] * scaled[j]
            tiles[later] = rest
    return jnp.concatenate(solved, axis=0)


def twice(factor):
    high, low = (part.astype(F32) for part in split(factor, 2))
    left = jnp.concatenate([high, low], axis=0)
    return jnp.concatenate([left, left], axis=1).astype(BF16)


def times(left, pair):
    product = lax.dot_general(left, pair, NN, preferred_element_type=F32)
    half = left.shape[0] // 2
    return product[:half] + product[half:]


def multiply(factor, pairs_ref, first, out_refs):
    ranks, span, lanes = out_refs[0].shape
    left = twice(factor)
    flat = [ref.reshape(ranks * span, lanes) for ref in out_refs]
    for pair in range(span // 2):
        product = times(left, pairs_ref[first + pair])
        for q in range(2):
            for d, ref in enumerate(flat):
                ref[pl.ds(2 * pair + q, ranks, stride=span), :] = product[
                    d * ranks : (d + 1) * ranks, q * lanes : (q + 1) * lanes
                ]


def solve_kernel(axis, sketch_ref, pairs_ref, factor_ref, *out_refs):
    rows = pairs_ref.shape[1] // 2
    sketch = sketch_ref[...]
    gram = lax.dot_general(sketch, sketch, NT, precision=PRECISE, preferred_element_type=F32)
    factor = eliminate(gram, sketch[:, :rows])
    parties = len(out_refs) + 1
    ranks = factor.shape[0] // parties
    me = lax.axis_index(axis)
    ordered = []
    for d in range(parties):
        rank_rows = factor[:ranks]
        for e in range(1, parties):
            rank_rows = jnp.where((me ^ d) == e, factor[e * ranks : (e + 1) * ranks], rank_rows)
        ordered.append(rank_rows)
    factor_ref[...] = jnp.concatenate(ordered, axis=0)
    multiply(jnp.concatenate(ordered[1:], axis=0), pairs_ref, 0, out_refs)


def ranks_kernel(first, begin, factor_ref, pairs_ref, *out_refs):
    ranks = out_refs[0].shape[0]
    multiply(factor_ref[begin : begin + ranks * len(out_refs), :], pairs_ref, first, out_refs)


def add_kernel(parties, own_ref, *refs):
    *others, out_hbm, total_ref, sems = refs
    copies, place = [], 0
    for chunk in range(len(others) // (parties - 1)):
        parts = others[chunk * (parties - 1) : (chunk + 1) * (parties - 1)]
        here = pl.ds(place, parts[0].shape[1])
        total = own_ref[:, here, :]
        for part in parts:
            total = total + part[...]
        total_ref[:, here, :] = total
        copies.append(pltpu.make_async_copy(total_ref.at[:, here], out_hbm.at[:, here], sems.at[chunk]))
        copies[-1].start()
        place += parts[0].shape[1]
    for copy in copies:
        copy.wait()


PARAMS = pltpu.CompilerParams(vmem_limit_bytes=VMEM_LIMIT)
COST = pl.CostEstimate(flops=1 << 30, bytes_accessed=1 << 25, transcendentals=0)


def project(sketch, pairs, sizes, spans):
    parties = sizes["gx"]
    columns, rows = sketch.shape[0], pairs.shape[1] // 2
    lanes = pairs.shape[2] // 2
    ranks, second = columns // parties, 2 * pairs.shape[0]
    chunks = [jax.ShapeDtypeStruct((ranks, span, lanes), F32) for span in spans]
    factor, *sent = pl.pallas_call(
        functools.partial(solve_kernel, "gx"),
        out_shape=[jax.ShapeDtypeStruct((columns, rows), F32)] + [chunks[0]] * (parties - 1),
        compiler_params=PARAMS,
        cost_estimate=COST,
        name="solve",
    )(sketch, pairs)
    received = [exchange(x, sizes, gx=d + 1) for d, x in enumerate(sent)]
    place = spans[0]
    for chunk in chunks[1:]:
        sent = pl.pallas_call(
            functools.partial(ranks_kernel, place // 2, ranks),
            out_shape=[chunk] * (parties - 1),
            compiler_params=PARAMS,
            cost_estimate=COST,
            name="others_ranks",
        )(factor, pairs)
        received += [exchange(x, sizes, gx=d + 1) for d, x in enumerate(sent)]
        place += chunk.shape[1]
    own = jax.ShapeDtypeStruct((ranks, second, lanes), F32)
    (core,) = pl.pallas_call(
        functools.partial(ranks_kernel, 0, 0),
        out_shape=[own],
        compiler_params=PARAMS,
        cost_estimate=pl.CostEstimate(flops=1 << 20, bytes_accessed=1 << 22, transcendentals=0),
        name="own_ranks",
    )(factor, pairs)
    return pl.pallas_call(
        functools.partial(add_kernel, parties),
        out_shape=own,
        out_specs=pl.BlockSpec(memory_space=pl.ANY),
        scratch_shapes=[pltpu.VMEM(own.shape, F32), pltpu.SemaphoreType.DMA((len(chunks),))],
        compiler_params=PARAMS,
        name="add_ranks",
    )(core, *received)


AXES = ("gx", "gy", "gz")


def exchange(x, sizes, **bits):
    order = [(gx, gy, gz) for gx in range(sizes["gx"]) for gy in range(sizes["gy"]) for gz in range(sizes["gz"])]
    place = {index: at for at, index in enumerate(order)}
    moves = [bits.get(axis, 0) for axis in AXES]
    pairs = [(at, place[tuple(i ^ move for i, move in zip(index, moves))]) for at, index in enumerate(order)]
    return lax.ppermute(x, AXES, pairs)


def steps_of(size):
    return [1 << b for b in range(size.bit_length() - 1)]


def body(sizes, field, test):
    second = field.shape[1]
    sketch, pairs = partial_sketch(field, test)
    for bit in steps_of(sizes["gz"]):
        sketch = sketch + exchange(sketch, sizes, gz=bit | 1)
    for bit in steps_of(sizes["gy"]):
        sketch = sketch + exchange(sketch, sizes, gy=bit)
    for bit in steps_of(sizes["gx"]):
        sketch = jnp.concatenate([sketch, exchange(sketch, sizes, gx=bit)], axis=1)
    return project(sketch, pairs, sizes, (3 * second // 4, second // 4))


def solution(mesh):
    in_specs = (P("gx", "gy", "gz"), P(None, "gy", "gz"))
    out_specs = P("gx", "gy", "gz")
    step = functools.partial(body, dict(mesh.shape))
    return jax.shard_map(step, mesh=mesh, in_specs=in_specs, out_specs=out_specs, check_vma=False)
```

```python
import functools

import jax
import jax.numpy as jnp
from jax import lax
from jax.experimental import pallas as pl
from jax.experimental.pallas import tpu as pltpu
from jax.sharding import PartitionSpec as P

F32, BF16 = jnp.float32, jnp.bfloat16
PRECISE = lax.Precision.HIGHEST
NT = (((1,), (1,)), ((), ()))
NN = (((1,), (0,)), ((), ()))
LANES, SUBLANES = 128, 8
VMEM_LIMIT = 48 << 20


def split(x, parts):
    terms = []
    for _ in range(parts - 1):
        terms.append(x.astype(BF16))
        x = x - terms[-1].astype(F32)
    return terms + [x.astype(BF16)]


def sketch_kernel(span, field_hbm, test_hbm, sketch_ref, pairs_ref, field, test, sems):
    rows, second, lanes = field_hbm.shape
    columns = test_hbm.shape[0]
    steps = second // span
    copies = []
    for step in range(steps):
        part = pl.ds(step * span, span)
        for which, (source, target) in enumerate(((field_hbm, field), (test_hbm, test))):
            copy = pltpu.make_async_copy(source.at[:, part], target.at[step], sems.at[which, step])
            copy.start()
            copies.append(copy)
    total = low = None
    for step in range(steps):
        copies[2 * step].wait()
        copies[2 * step + 1].wait()
        flat_field = field.at[step].reshape(rows * span, lanes)
        flat_test = test.at[step].reshape(columns * span, lanes)
        for pair in range(span // 2):
            x = jnp.concatenate([flat_field[pl.ds(2 * pair + q, rows, stride=span), :] for q in range(2)], axis=1)
            t = jnp.concatenate([flat_test[pl.ds(2 * pair + q, columns, stride=span), :] for q in range(2)], axis=1)
            x = split(x, 3)
            t = split(t, 3)
            weights = jnp.concatenate(x[:2], axis=0)
            pairs_ref[step * span // 2 + pair] = weights
            term = lax.dot_general(jnp.concatenate(t, axis=0), weights, NT, preferred_element_type=F32)
            rest = lax.dot_general(t[0], x[2], NT, preferred_element_type=F32)
            total = term if total is None else total + term
            low = rest if low is None else low + rest
    for part in reversed(range(3)):
        block = total[part * columns : (part + 1) * columns]
        low = low + block[:, rows:] + block[:, :rows] if part else (low + block[:, rows:]) + block[:, :rows]
    sketch_ref[...] = low


def partial_sketch(field, test):
    rows, second, lanes = field.shape
    columns = test.shape[0]
    span = SUBLANES
    steps = second // span
    return pl.pallas_call(
        functools.partial(sketch_kernel, span),
        in_specs=[pl.BlockSpec(memory_space=pl.ANY)] * 2,
        out_shape=[
            jax.ShapeDtypeStruct((columns, rows), F32),
            jax.ShapeDtypeStruct((second // 2, 2 * rows, 2 * lanes), BF16),
        ],
        scratch_shapes=[
            pltpu.VMEM((steps, rows, span, lanes), F32),
            pltpu.VMEM((steps, columns, span, lanes), F32),
            pltpu.SemaphoreType.DMA((2, steps)),
        ],
        compiler_params=pltpu.CompilerParams(vmem_limit_bytes=VMEM_LIMIT),
        name="partial_sketch",
    )(*(pltpu.with_memory_space_constraint(array, pltpu.HBM) for array in (field, test)))


def eliminate(gram, right, spread_ref):
    size, width = gram.shape[0], LANES + right.shape[1]
    whole = jnp.concatenate([gram, jnp.zeros((size, LANES - size), F32), right], axis=1)
    tiles = [whole[i : i + SUBLANES] for i in range(0, size, SUBLANES)]
    spread = lambda x: jnp.broadcast_to(x, (SUBLANES, LANES))
    widen = lambda x: jnp.concatenate([x] * (width // LANES), axis=1)
    block = range(SUBLANES)
    solved = []
    for t, tile in enumerate(tiles):
        start = t * SUBLANES
        for j in block:
            spread_ref[t, j] = spread(tile[:, start + j : start + j + 1])
        entry = {(i, j): spread(spread_ref[t, j, i : i + 1, :]) for j in block for i in range(j, SUBLANES)}
        inverse, lower = [], {}
        for j in block:
            inverse.append(1.0 / entry[j, j])
            for i in range(j + 1, SUBLANES):
                lower[i, j] = entry[i, j] * inverse[j]
            for m in range(j + 1, SUBLANES):
                for i in range(m, SUBLANES):
                    entry[i, m] = entry[i, m] - lower[i, j] * entry[m, j]
        lower = {at: widen(x) for at, x in lower.items()}
        reduced = []
        for i in block:
            row = jnp.broadcast_to(tile[i : i + 1], (SUBLANES, width))
            for j in range(i):
                row = row - lower[i, j] * reduced[j]
            reduced.append(row)
            solved.append(row[:1, LANES:] * widen(lax.rsqrt(entry[i, i]))[:1, LANES:])
        if t == len(tiles) - 1:
            break
        scaled = [None] * SUBLANES
        for i in reversed(block):
            row = reduced[i] * widen(inverse[i])
            for j in range(i + 1, SUBLANES):
                row = row - lower[j, i] * scaled[j]
            scaled[i] = row
        for later in range(t + 1, len(tiles)):
            rest = tiles[later]
            for j in block:
                rest = rest - tiles[later][:, start + j : start + j + 1] * scaled[j]
            tiles[later] = rest
    return jnp.concatenate(solved, axis=0)


def twice(factor):
    high, low = (part.astype(F32) for part in split(factor, 2))
    left = jnp.concatenate([high, low], axis=0)
    return jnp.concatenate([left, left], axis=1).astype(BF16)


def times(left, pair):
    product = lax.dot_general(left, pair, NN, preferred_element_type=F32)
    half = left.shape[0] // 2
    return product[:half] + product[half:]


def multiply(factor, pairs_ref, first, out_refs):
    ranks, span, lanes = out_refs[0].shape
    left = twice(factor)
    flat = [ref.reshape(ranks * span, lanes) for ref in out_refs]
    for pair in range(span // 2):
        product = times(left, pairs_ref[first + pair])
        for q in range(2):
            for d, ref in enumerate(flat):
                ref[pl.ds(2 * pair + q, ranks, stride=span), :] = product[
                    d * ranks : (d + 1) * ranks, q * lanes : (q + 1) * lanes
                ]


def solve_kernel(axis, sketch_ref, pairs_ref, factor_ref, *refs):
    *out_refs, spread_ref = refs
    rows = pairs_ref.shape[1] // 2
    sketch = sketch_ref[...]
    gram = lax.dot_general(sketch, sketch, NT, precision=PRECISE, preferred_element_type=F32)
    factor = eliminate(gram, sketch[:, :rows], spread_ref)
    parties = len(out_refs) + 1
    ranks = factor.shape[0] // parties
    me = lax.axis_index(axis)
    ordered = []
    for d in range(parties):
        rank_rows = factor[:ranks]
        for e in range(1, parties):
            rank_rows = jnp.where((me ^ d) == e, factor[e * ranks : (e + 1) * ranks], rank_rows)
        ordered.append(rank_rows)
    factor_ref[...] = jnp.concatenate(ordered, axis=0)
    multiply(jnp.concatenate(ordered[1:], axis=0), pairs_ref, 0, out_refs)


def ranks_kernel(first, begin, factor_ref, pairs_ref, *out_refs):
    ranks = out_refs[0].shape[0]
    multiply(factor_ref[begin : begin + ranks * len(out_refs), :], pairs_ref, first, out_refs)


def add_kernel(parties, own_ref, *refs):
    *others, out_hbm, total_ref, sems = refs
    copies, place = [], 0
    for chunk in range(len(others) // (parties - 1)):
        parts = others[chunk * (parties - 1) : (chunk + 1) * (parties - 1)]
        here = pl.ds(place, parts[0].shape[1])
        total = own_ref[:, here, :]
        for part in parts:
            total = total + part[...]
        total_ref[:, here, :] = total
        copies.append(pltpu.make_async_copy(total_ref.at[:, here], out_hbm.at[:, here], sems.at[chunk]))
        copies[-1].start()
        place += parts[0].shape[1]
    for copy in copies:
        copy.wait()


PARAMS = pltpu.CompilerParams(vmem_limit_bytes=VMEM_LIMIT)
COST = pl.CostEstimate(flops=1 << 30, bytes_accessed=1 << 25, transcendentals=0)


def project(sketch, pairs, sizes, spans):
    parties = sizes["gx"]
    columns, rows = sketch.shape[0], pairs.shape[1] // 2
    lanes = pairs.shape[2] // 2
    ranks, second = columns // parties, 2 * pairs.shape[0]
    chunks = [jax.ShapeDtypeStruct((ranks, span, lanes), F32) for span in spans]
    factor, *sent = pl.pallas_call(
        functools.partial(solve_kernel, "gx"),
        out_shape=[jax.ShapeDtypeStruct((columns, rows), F32)] + [chunks[0]] * (parties - 1),
        scratch_shapes=[pltpu.VMEM((columns // SUBLANES, SUBLANES, SUBLANES, LANES), F32)],
        compiler_params=PARAMS,
        cost_estimate=COST,
        name="solve",
    )(sketch, pairs)
    received = [exchange(x, sizes, gx=d + 1) for d, x in enumerate(sent)]
    place = spans[0]
    for chunk in chunks[1:]:
        sent = pl.pallas_call(
            functools.partial(ranks_kernel, place // 2, ranks),
            out_shape=[chunk] * (parties - 1),
            compiler_params=PARAMS,
            cost_estimate=COST,
            name="others_ranks",
        )(factor, pairs)
        received += [exchange(x, sizes, gx=d + 1) for d, x in enumerate(sent)]
        place += chunk.shape[1]
    own = jax.ShapeDtypeStruct((ranks, second, lanes), F32)
    (core,) = pl.pallas_call(
        functools.partial(ranks_kernel, 0, 0),
        out_shape=[own],
        compiler_params=PARAMS,
        cost_estimate=pl.CostEstimate(flops=1 << 20, bytes_accessed=1 << 22, transcendentals=0),
        name="own_ranks",
    )(factor, pairs)
    return pl.pallas_call(
        functools.partial(add_kernel, parties),
        out_shape=own,
        out_specs=pl.BlockSpec(memory_space=pl.ANY),
        scratch_shapes=[pltpu.VMEM(own.shape, F32), pltpu.SemaphoreType.DMA((len(chunks),))],
        compiler_params=PARAMS,
        name="add_ranks",
    )(core, *received)


AXES = ("gx", "gy", "gz")


def exchange(x, sizes, **bits):
    order = [(gx, gy, gz) for gx in range(sizes["gx"]) for gy in range(sizes["gy"]) for gz in range(sizes["gz"])]
    place = {index: at for at, index in enumerate(order)}
    moves = [bits.get(axis, 0) for axis in AXES]
    pairs = [(at, place[tuple(i ^ move for i, move in zip(index, moves))]) for at, index in enumerate(order)]
    return lax.ppermute(x, AXES, pairs)


def steps_of(size):
    return [1 << b for b in range(size.bit_length() - 1)]


def body(sizes, field, test):
    second = field.shape[1]
    sketch, pairs = partial_sketch(field, test)
    for bit in steps_of(sizes["gz"]):
        sketch = sketch + exchange(sketch, sizes, gz=bit | 1)
    for bit in steps_of(sizes["gy"]):
        sketch = sketch + exchange(sketch, sizes, gy=bit)
    for bit in steps_of(sizes["gx"]):
        sketch = jnp.concatenate([sketch, exchange(sketch, sizes, gx=bit)], axis=1)
    return project(sketch, pairs, sizes, (3 * second // 4, second // 4))


def solution(mesh):
    in_specs = (P("gx", "gy", "gz"), P(None, "gy", "gz"))
    out_specs = P("gx", "gy", "gz")
    step = functools.partial(body, dict(mesh.shape))
    return jax.shard_map(step, mesh=mesh, in_specs=in_specs, out_specs=out_specs, check_vma=False)
```

```python
import functools

import jax
import jax.numpy as jnp
from jax import lax
from jax.experimental import pallas as pl
from jax.experimental.pallas import tpu as pltpu
from jax.sharding import PartitionSpec as P

F32, BF16 = jnp.float32, jnp.bfloat16
PRECISE = lax.Precision.HIGHEST
NT = (((1,), (1,)), ((), ()))
NN = (((1,), (0,)), ((), ()))
LANES, SUBLANES = 128, 8
VMEM_LIMIT = 48 << 20


def split(x, parts):
    terms = []
    for _ in range(parts - 1):
        terms.append(x.astype(BF16))
        x = x - terms[-1].astype(F32)
    return terms + [x.astype(BF16)]


def sketch_kernel(span, field_hbm, test_hbm, sketch_ref, pairs_ref, field, test, sems):
    rows, second, lanes = field_hbm.shape
    columns = test_hbm.shape[0]
    steps = second // span
    copies = []
    for step in range(steps):
        part = pl.ds(step * span, span)
        for which, (source, target) in enumerate(((field_hbm, field), (test_hbm, test))):
            copy = pltpu.make_async_copy(source.at[:, part], target.at[step], sems.at[which, step])
            copy.start()
            copies.append(copy)
    total = low = None
    for step in range(steps):
        copies[2 * step].wait()
        copies[2 * step + 1].wait()
        flat_field = field.at[step].reshape(rows * span, lanes)
        flat_test = test.at[step].reshape(columns * span, lanes)
        for pair in range(span // 2):
            x = jnp.concatenate([flat_field[pl.ds(2 * pair + q, rows, stride=span), :] for q in range(2)], axis=1)
            t = jnp.concatenate([flat_test[pl.ds(2 * pair + q, columns, stride=span), :] for q in range(2)], axis=1)
            x = split(x, 3)
            t = split(t, 3)
            weights = jnp.concatenate(x[:2], axis=0)
            pairs_ref[step * span // 2 + pair] = weights
            term = lax.dot_general(jnp.concatenate(t, axis=0), weights, NT, preferred_element_type=F32)
            rest = lax.dot_general(t[0], x[2], NT, preferred_element_type=F32)
            total = term if total is None else total + term
            low = rest if low is None else low + rest
    for part in reversed(range(3)):
        block = total[part * columns : (part + 1) * columns]
        low = low + block[:, rows:] + block[:, :rows] if part else (low + block[:, rows:]) + block[:, :rows]
    sketch_ref[...] = low


def partial_sketch(field, test):
    rows, second, lanes = field.shape
    columns = test.shape[0]
    span = SUBLANES
    steps = second // span
    return pl.pallas_call(
        functools.partial(sketch_kernel, span),
        in_specs=[pl.BlockSpec(memory_space=pl.ANY)] * 2,
        out_shape=[
            jax.ShapeDtypeStruct((columns, rows), F32),
            jax.ShapeDtypeStruct((second // 2, 2 * rows, 2 * lanes), BF16),
        ],
        scratch_shapes=[
            pltpu.VMEM((steps, rows, span, lanes), F32),
            pltpu.VMEM((steps, columns, span, lanes), F32),
            pltpu.SemaphoreType.DMA((2, steps)),
        ],
        compiler_params=pltpu.CompilerParams(vmem_limit_bytes=VMEM_LIMIT),
        name="partial_sketch",
    )(*(pltpu.with_memory_space_constraint(array, pltpu.HBM) for array in (field, test)))


def unit(size):
    return jnp.where(
        lax.broadcasted_iota(jnp.int32, (size, size), 0) == lax.broadcasted_iota(jnp.int32, (size, size), 1), 1.0, 0.0
    ).astype(F32)


def eliminate(gram, right, spread_ref):
    size, width = gram.shape[0], LANES + right.shape[1]
    whole = jnp.concatenate([unit(size), gram, jnp.zeros((size, LANES - 2 * size), F32), right], axis=1)
    tiles = [whole[i : i + SUBLANES] for i in range(0, size, SUBLANES)]
    spread = lambda x: jnp.broadcast_to(x, (SUBLANES, LANES))
    widen = lambda x: jnp.concatenate([x] * (width // LANES), axis=1)
    block = range(SUBLANES)
    solved = []
    for t, tile in enumerate(tiles):
        start = size + t * SUBLANES
        for j in block:
            spread_ref[t, j] = spread(tile[:, start + j : start + j + 1])
        entry = {(i, j): spread(spread_ref[t, j, i : i + 1, :]) for j in block for i in range(j, SUBLANES)}
        inverse, lower = [], {}
        for j in block:
            inverse.append(1.0 / entry[j, j])
            for i in range(j + 1, SUBLANES):
                lower[i, j] = entry[i, j] * inverse[j]
            for m in range(j + 1, SUBLANES):
                for i in range(m, SUBLANES):
                    entry[i, m] = entry[i, m] - lower[i, j] * entry[m, j]
        lower = {at: widen(x) for at, x in lower.items()}
        reduced = []
        for i in block:
            row = jnp.broadcast_to(tile[i : i + 1], (SUBLANES, width))
            for j in range(i):
                row = row - lower[i, j] * reduced[j]
            reduced.append(row)
            solved.append((row * widen(lax.rsqrt(entry[i, i])))[:1])
        if t == len(tiles) - 1:
            break
        scaled = [None] * SUBLANES
        for i in reversed(block):
            row = reduced[i] * widen(inverse[i])
            for j in range(i + 1, SUBLANES):
                row = row - lower[j, i] * scaled[j]
            scaled[i] = row
        for later in range(t + 1, len(tiles)):
            rest = tiles[later]
            for j in block:
                rest = rest - tiles[later][:, start + j : start + j + 1] * scaled[j]
            tiles[later] = rest
    return jnp.concatenate(solved, axis=0)


def twice(factor):
    high, low = (part.astype(F32) for part in split(factor, 2))
    left = jnp.concatenate([high, low], axis=0)
    return jnp.concatenate([left, left], axis=1).astype(BF16)


def times(left, pair):
    product = lax.dot_general(left, pair, NN, preferred_element_type=F32)
    half = left.shape[0] // 2
    return product[:half] + product[half:]


def multiply(factor, pairs_ref, first, out_refs, begin=0):
    span, ranks, lanes = out_refs[0].shape
    left = twice(factor)
    for pair in range((span - begin) // 2):
        product = times(left, pairs_ref[first + pair])
        for q in range(2):
            for d, ref in enumerate(out_refs):
                ref[begin + 2 * pair + q] = product[d * ranks : (d + 1) * ranks, q * lanes : (q + 1) * lanes]


def raw_kernel(sketch_ref, pairs_ref, out_ref):
    multiply(sketch_ref[...], pairs_ref, 0, [out_ref])


def solve_kernel(axis, first, sketch_ref, pairs_ref, solved_ref, *refs):
    *out_refs, spread_ref = refs
    rows = pairs_ref.shape[1] // 2
    sketch = sketch_ref[...]
    gram = lax.dot_general(sketch, sketch, NT, precision=PRECISE, preferred_element_type=F32)
    solved = eliminate(gram, sketch[:, :rows], spread_ref)
    parties = len(out_refs) + 1
    ranks = solved.shape[0] // parties
    me = lax.axis_index(axis)
    ordered = []
    for d in range(parties):
        rank_rows = solved[:ranks]
        for e in range(1, parties):
            rank_rows = jnp.where((me ^ d) == e, solved[e * ranks : (e + 1) * ranks], rank_rows)
        ordered.append(rank_rows)
    solved_ref[...] = jnp.concatenate(ordered, axis=0)
    multiply(jnp.concatenate(ordered[1:], axis=0)[:, LANES:], pairs_ref, first, out_refs)


def others_kernel(first, solved_ref, pairs_ref, *out_refs):
    ranks = out_refs[0].shape[1]
    multiply(solved_ref[ranks : ranks * (1 + len(out_refs)), LANES:], pairs_ref, first, out_refs)


def own_kernel(first, solved_ref, pairs_ref, *refs):
    *raw_refs, out_ref = refs
    span, ranks, lanes = out_ref.shape
    solved = solved_ref[:ranks, :]
    multiply(solved[:, LANES:], pairs_ref, first, [out_ref], 2 * first)
    for pair in range(first):
        right = []
        for at in (2 * pair, 2 * pair + 1):
            total = raw_refs[0][at]
            for ref in raw_refs[1:]:
                total = total + ref[at]
            right.append(total)
        columns = right[0].shape[0]
        product = lax.dot_general(
            solved[:, :columns], jnp.concatenate(right, axis=1), NN, precision=PRECISE, preferred_element_type=F32
        )
        for q in range(2):
            out_ref[2 * pair + q] = product[:, q * lanes : (q + 1) * lanes]


def add_kernel(parties, begin, size, own_ref, *refs):
    *others, out_hbm, total_ref, sem = refs
    others = others[: parties - 1]
    ranks, span, lanes = total_ref.shape
    flat = total_ref.reshape(ranks * span, lanes)
    bare = size - others[0].shape[0]
    for at in range(size):
        total = own_ref[begin + at]
        for part in others if at >= bare else ():
            total = total + part[at - bare]
        flat[pl.ds(at, ranks, stride=span), :] = total
    copy = pltpu.make_async_copy(total_ref, out_hbm.at[:, pl.ds(begin, size)], sem)
    copy.start()
    copy.wait()


PARAMS = pltpu.CompilerParams(vmem_limit_bytes=VMEM_LIMIT)
COST = pl.CostEstimate(flops=1 << 30, bytes_accessed=1 << 25, transcendentals=0)


def run(kernel, name, out_shape, *operands, cost=COST, scratch=()):
    return pl.pallas_call(
        kernel, out_shape=out_shape, compiler_params=PARAMS, cost_estimate=cost, name=name, scratch_shapes=scratch
    )(*operands)


def project(sketch, pairs, sizes, raw, spans):
    parties = sizes["gx"]
    columns, rows = sketch.shape[0], pairs.shape[1] // 2
    lanes = pairs.shape[2] // 2
    ranks, second = columns // parties, 2 * pairs.shape[0]
    piece = lambda span, height: jax.ShapeDtypeStruct((span, height, lanes), F32)
    whole = sketch
    for bit in steps_of(parties):
        whole = jnp.concatenate([whole, exchange(whole, sizes, gx=bit)], axis=1)
    raw_parts = []
    if raw:
        mine = run(raw_kernel, "raw_product", piece(raw, columns), sketch, pairs)
        raw_parts = [mine] + [exchange(mine, sizes, gx=d) for d in range(1, parties)]
    place, received = raw, []
    solved, *sent = run(
        functools.partial(solve_kernel, "gx", place // 2),
        "solve",
        [jax.ShapeDtypeStruct((columns, LANES + rows), F32)] + [piece(spans[0], ranks)] * (parties - 1),
        whole,
        pairs,
        scratch=[pltpu.VMEM((columns // SUBLANES, SUBLANES, SUBLANES, LANES), F32)],
    )
    for step, span in enumerate(spans):
        if step:
            sent = run(
                functools.partial(others_kernel, place // 2),
                "others_ranks",
                [piece(span, ranks)] * (parties - 1),
                solved,
                pairs,
            )
        received += [exchange(x, sizes, gx=d + 1) for d, x in enumerate(sent)]
        place += span
    core = run(functools.partial(own_kernel, raw // 2), "own_ranks", piece(second, ranks), solved, pairs, *raw_parts)
    out, begin = None, 0
    for step, span in enumerate(spans):
        size = span if step else raw + span
        whole_before = [] if out is None else [out]
        count = 1 + (parties - 1)
        parts = received[step * (parties - 1) : (step + 1) * (parties - 1)]
        out = pl.pallas_call(
            functools.partial(add_kernel, parties, begin, size),
            out_shape=jax.ShapeDtypeStruct((ranks, second, lanes), F32),
            in_specs=[pl.BlockSpec(memory_space=pltpu.VMEM)] * count + [pl.BlockSpec(memory_space=pl.ANY)] * len(whole_before),
            out_specs=pl.BlockSpec(memory_space=pl.ANY),
            input_output_aliases={count: 0} if whole_before else {},
            scratch_shapes=[pltpu.VMEM((ranks, size, lanes), F32), pltpu.SemaphoreType.DMA],
            compiler_params=PARAMS,
            cost_estimate=COST if step < len(spans) - 1 else None,
            name="add_ranks",
        )(core, *parts, *whole_before)
        begin += size
    return out


AXES = ("gx", "gy", "gz")


def exchange(x, sizes, **bits):
    order = [(gx, gy, gz) for gx in range(sizes["gx"]) for gy in range(sizes["gy"]) for gz in range(sizes["gz"])]
    place = {index: at for at, index in enumerate(order)}
    moves = [bits.get(axis, 0) for axis in AXES]
    pairs = [(at, place[tuple(i ^ move for i, move in zip(index, moves))]) for at, index in enumerate(order)]
    return lax.ppermute(x, AXES, pairs)


def steps_of(size):
    return [1 << b for b in range(size.bit_length() - 1)]


def body(sizes, field, test):
    second = field.shape[1]
    sketch, pairs = partial_sketch(field, test)
    for bit in steps_of(sizes["gz"]):
        sketch = sketch + exchange(sketch, sizes, gz=bit | 1)
    for bit in steps_of(sizes["gy"]):
        sketch = sketch + exchange(sketch, sizes, gy=bit, gz=1)
    raw, last = second * 3 // 16, second // 4
    return project(sketch, pairs, sizes, raw, (second - raw - last, last))


def solution(mesh):
    in_specs = (P("gx", "gy", "gz"), P(None, "gy", "gz"))
    out_specs = P("gx", "gy", "gz")
    step = functools.partial(body, dict(mesh.shape))
    return jax.shard_map(step, mesh=mesh, in_specs=in_specs, out_specs=out_specs, check_vma=False)
```

```python
import functools

import jax
import jax.numpy as jnp
from jax import lax
from jax.experimental import pallas as pl
from jax.experimental.pallas import tpu as pltpu
from jax.sharding import PartitionSpec as P

F32, BF16 = jnp.float32, jnp.bfloat16
PRECISE = lax.Precision.HIGHEST
NT = (((1,), (1,)), ((), ()))
NN = (((1,), (0,)), ((), ()))
LANES, SUBLANES = 128, 8
VMEM_LIMIT = 48 << 20


def split(x, parts):
    terms = []
    for _ in range(parts - 1):
        terms.append(x.astype(BF16))
        x = x - terms[-1].astype(F32)
    return terms + [x.astype(BF16)]


def sketch_kernel(span, field_hbm, test_hbm, sketch_ref, pairs_ref, first_ref, field, test, sems):
    rows, second, lanes = field_hbm.shape
    columns = test_hbm.shape[0]
    steps = second // span
    copies = []
    for step in range(steps):
        part = pl.ds(step * span, span)
        for which, (source, target) in enumerate(((field_hbm, field), (test_hbm, test))):
            copy = pltpu.make_async_copy(source.at[:, part], target.at[step], sems.at[which, step])
            copy.start()
            copies.append(copy)
    total = low = None
    for step in range(steps):
        copies[2 * step].wait()
        copies[2 * step + 1].wait()
        flat_field = field.at[step].reshape(rows * span, lanes)
        flat_test = test.at[step].reshape(columns * span, lanes)
        for pair in range(span // 2):
            x = [flat_field[pl.ds(2 * pair + q, rows, stride=span), :] for q in range(2)]
            for q in range(2):
                if step * span + 2 * pair + q < first_ref.shape[0]:
                    first_ref[step * span + 2 * pair + q] = x[q]
            x = jnp.concatenate(x, axis=1)
            t = jnp.concatenate([flat_test[pl.ds(2 * pair + q, columns, stride=span), :] for q in range(2)], axis=1)
            x = split(x, 3)
            t = split(t, 3)
            weights = jnp.concatenate(x[:2], axis=0)
            pairs_ref[step * span // 2 + pair] = weights
            term = lax.dot_general(jnp.concatenate(t, axis=0), weights, NT, preferred_element_type=F32)
            rest = lax.dot_general(t[0], x[2], NT, preferred_element_type=F32)
            total = term if total is None else total + term
            low = rest if low is None else low + rest
    for part in reversed(range(3)):
        block = total[part * columns : (part + 1) * columns]
        low = low + block[:, rows:] + block[:, :rows] if part else (low + block[:, rows:]) + block[:, :rows]
    sketch_ref[...] = low


def partial_sketch(field, test, first):
    rows, second, lanes = field.shape
    columns = test.shape[0]
    span = SUBLANES
    steps = second // span
    return pl.pallas_call(
        functools.partial(sketch_kernel, span),
        in_specs=[pl.BlockSpec(memory_space=pl.ANY)] * 2,
        out_shape=[
            jax.ShapeDtypeStruct((columns, rows), F32),
            jax.ShapeDtypeStruct((second // 2, 2 * rows, 2 * lanes), BF16),
            jax.ShapeDtypeStruct((first, rows, lanes), F32),
        ],
        scratch_shapes=[
            pltpu.VMEM((steps, rows, span, lanes), F32),
            pltpu.VMEM((steps, columns, span, lanes), F32),
            pltpu.SemaphoreType.DMA((2, steps)),
        ],
        compiler_params=pltpu.CompilerParams(vmem_limit_bytes=VMEM_LIMIT),
        name="partial_sketch",
    )(*(pltpu.with_memory_space_constraint(array, pltpu.HBM) for array in (field, test)))


def unit(size):
    return jnp.where(
        lax.broadcasted_iota(jnp.int32, (size, size), 0) == lax.broadcasted_iota(jnp.int32, (size, size), 1), 1.0, 0.0
    ).astype(F32)


def eliminate(gram, right, spread_ref):
    size, width = gram.shape[0], LANES + right.shape[1]
    whole = jnp.concatenate([unit(size), gram, jnp.zeros((size, LANES - 2 * size), F32), right], axis=1)
    tiles = [whole[i : i + SUBLANES] for i in range(0, size, SUBLANES)]
    spread = lambda x: jnp.broadcast_to(x, (SUBLANES, LANES))
    widen = lambda x: jnp.concatenate([x] * (width // LANES), axis=1)
    block = range(SUBLANES)
    solved = []
    for t, tile in enumerate(tiles):
        start = size + t * SUBLANES
        for j in block:
            spread_ref[t, j] = spread(tile[:, start + j : start + j + 1])
        entry = {(i, j): spread(spread_ref[t, j, i : i + 1, :]) for j in block for i in range(j, SUBLANES)}
        inverse, lower = [], {}
        for j in block:
            inverse.append(1.0 / entry[j, j])
            for i in range(j + 1, SUBLANES):
                lower[i, j] = entry[i, j] * inverse[j]
            for m in range(j + 1, SUBLANES):
                for i in range(m, SUBLANES):
                    entry[i, m] = entry[i, m] - lower[i, j] * entry[m, j]
        lower = {at: widen(x) for at, x in lower.items()}
        reduced = []
        for i in block:
            row = jnp.broadcast_to(tile[i : i + 1], (SUBLANES, width))
            for j in range(i):
                row = row - lower[i, j] * reduced[j]
            reduced.append(row)
            solved.append((row * widen(lax.rsqrt(entry[i, i])))[:1])
        if t == len(tiles) - 1:
            break
        scaled = [None] * SUBLANES
        for i in reversed(block):
            row = reduced[i] * widen(inverse[i])
            for j in range(i + 1, SUBLANES):
                row = row - lower[j, i] * scaled[j]
            scaled[i] = row
        for later in range(t + 1, len(tiles)):
            rest = tiles[later]
            for j in block:
                rest = rest - tiles[later][:, start + j : start + j + 1] * scaled[j]
            tiles[later] = rest
    return jnp.concatenate(solved, axis=0)


def twice(factor):
    high, low = (part.astype(F32) for part in split(factor, 2))
    left = jnp.concatenate([high, low], axis=0)
    return jnp.concatenate([left, left], axis=1).astype(BF16)


def times(left, pair):
    product = lax.dot_general(left, pair, NN, preferred_element_type=F32)
    half = left.shape[0] // 2
    return product[:half] + product[half:]


def multiply(factor, pairs_ref, first, out_refs, begin=0):
    span, ranks, lanes = out_refs[0].shape
    left = twice(factor)
    for pair in range((span - begin) // 2):
        product = times(left, pairs_ref[first + pair])
        for q in range(2):
            for d, ref in enumerate(out_refs):
                ref[begin + 2 * pair + q] = product[d * ranks : (d + 1) * ranks, q * lanes : (q + 1) * lanes]


def copy_kernel(sketch_ref, field_ref, out_ref):
    out_ref[...] = field_ref[...]


def raw_kernel(first, sketch_ref, pairs_ref, out_ref):
    multiply(sketch_ref[...], pairs_ref, first, [out_ref])


def solve_kernel(axis, first, sketch_ref, pairs_ref, solved_ref, *refs):
    *out_refs, spread_ref = refs
    rows = pairs_ref.shape[1] // 2
    sketch = sketch_ref[...]
    gram = lax.dot_general(sketch, sketch, NT, precision=PRECISE, preferred_element_type=F32)
    solved = eliminate(gram, sketch[:, :rows], spread_ref)
    parties = len(out_refs) + 1
    ranks = solved.shape[0] // parties
    me = lax.axis_index(axis)
    ordered = []
    for d in range(parties):
        rank_rows = solved[:ranks]
        for e in range(1, parties):
            rank_rows = jnp.where((me ^ d) == e, solved[e * ranks : (e + 1) * ranks], rank_rows)
        ordered.append(rank_rows)
    solved_ref[...] = jnp.concatenate(ordered, axis=0)
    multiply(jnp.concatenate(ordered[1:], axis=0)[:, LANES:], pairs_ref, first, out_refs)


def others_kernel(first, solved_ref, pairs_ref, *out_refs):
    ranks = out_refs[0].shape[1]
    multiply(solved_ref[ranks : ranks * (1 + len(out_refs)), LANES:], pairs_ref, first, out_refs)


def own_kernel(parties, whole_pairs, raw_pairs, sketch_ref, solved_ref, pairs_ref, *refs):
    *refs, out_ref = refs
    field_refs, raw_refs = refs[: parties - 1], refs[parties - 1 :]
    span, ranks, lanes = out_ref.shape
    columns, rows = sketch_ref.shape[0], sketch_ref.shape[1] // parties
    solved = solved_ref[:ranks, :]
    inverse = solved[:, :columns]
    apply = functools.partial(lax.dot_general, dimension_numbers=NN, precision=PRECISE, preferred_element_type=F32)
    done = whole_pairs + raw_pairs
    multiply(solved[:, LANES:], pairs_ref, done, [out_ref], 2 * done)
    lefts = [twice(solved[:, LANES:])]
    lefts += [twice(apply(inverse, sketch_ref[:, d * rows : (d + 1) * rows])) for d in range(1, parties)]
    for pair in range(done):
        if pair < whole_pairs:
            product = times(lefts[0], pairs_ref[pair])
            for left, ref in zip(lefts[1:], field_refs):
                terms = split(jnp.concatenate([ref[2 * pair], ref[2 * pair + 1]], axis=1), 2)
                product = product + times(left, jnp.concatenate(terms, axis=0))
        else:
            right = []
            for at in (2 * (pair - whole_pairs), 2 * (pair - whole_pairs) + 1):
                total = raw_refs[0][at]
                for ref in raw_refs[1:]:
                    total = total + ref[at]
                right.append(total)
            product = apply(inverse, jnp.concatenate(right, axis=1))
        for q in range(2):
            out_ref[2 * pair + q] = product[:, q * lanes : (q + 1) * lanes]


def add_kernel(parties, begin, size, own_ref, *refs):
    *others, out_hbm, total_ref, sem = refs
    others = others[: parties - 1]
    ranks, span, lanes = total_ref.shape
    flat = total_ref.reshape(ranks * span, lanes)
    bare = size - others[0].shape[0]
    for at in range(size):
        total = own_ref[begin + at]
        for part in others if at >= bare else ():
            total = total + part[at - bare]
        flat[pl.ds(at, ranks, stride=span), :] = total
    copy = pltpu.make_async_copy(total_ref, out_hbm.at[:, pl.ds(begin, size)], sem)
    copy.start()
    copy.wait()


PARAMS = pltpu.CompilerParams(vmem_limit_bytes=VMEM_LIMIT)
COST = pl.CostEstimate(flops=1 << 30, bytes_accessed=1 << 25, transcendentals=0)


def run(kernel, name, out_shape, *operands, cost=COST, scratch=()):
    if isinstance(out_shape, jax.Array):
        out_shape = jax.ShapeDtypeStruct(out_shape.shape, out_shape.dtype)
    return pl.pallas_call(
        kernel, out_shape=out_shape, compiler_params=PARAMS, cost_estimate=cost, name=name, scratch_shapes=scratch
    )(*operands)


def project(sketch, pairs, first_field, sizes, raw, spans):
    parties = sizes["gx"]
    columns, rows = sketch.shape[0], pairs.shape[1] // 2
    lanes = pairs.shape[2] // 2
    ranks, second = columns // parties, 2 * pairs.shape[0]
    piece = lambda span, height: jax.ShapeDtypeStruct((span, height, lanes), F32)
    early = first_field.shape[0]
    fields = [exchange(first_field, sizes, gx=d) for d in range(1, parties)]
    whole = sketch
    summed = whole
    for bit in steps_of(parties):
        whole = jnp.concatenate([whole, exchange(whole, sizes, gx=bit)], axis=1)
    mine = run(functools.partial(raw_kernel, early // 2), "raw_product", piece(raw, columns), summed, pairs)
    raw_parts = [mine] + [exchange(mine, sizes, gx=d) for d in range(1, parties)]
    whole, *fields = lax.optimization_barrier([whole, *fields])
    place, received = early + raw, []
    solved, *sent = run(
        functools.partial(solve_kernel, "gx", place // 2),
        "solve",
        [jax.ShapeDtypeStruct((columns, LANES + rows), F32)] + [piece(spans[0], ranks)] * (parties - 1),
        whole,
        pairs,
        scratch=[pltpu.VMEM((columns // SUBLANES, SUBLANES, SUBLANES, LANES), F32)],
    )
    for step, span in enumerate(spans):
        if step:
            sent = run(
                functools.partial(others_kernel, place // 2),
                "others_ranks",
                [piece(span, ranks)] * (parties - 1),
                solved,
                pairs,
            )
        received += [exchange(x, sizes, gx=d + 1) for d, x in enumerate(sent)]
        place += span
    core = run(
        functools.partial(own_kernel, parties, early // 2, raw // 2),
        "own_ranks",
        piece(second, ranks),
        whole,
        solved,
        pairs,
        *fields,
        *raw_parts,
    )
    out, begin = None, 0
    for step, span in enumerate(spans):
        size = span if step else early + raw + span
        whole_before = [] if out is None else [out]
        count = 1 + (parties - 1)
        parts = received[step * (parties - 1) : (step + 1) * (parties - 1)]
        out = pl.pallas_call(
            functools.partial(add_kernel, parties, begin, size),
            out_shape=jax.ShapeDtypeStruct((ranks, second, lanes), F32),
            in_specs=[pl.BlockSpec(memory_space=pltpu.VMEM)] * count + [pl.BlockSpec(memory_space=pl.ANY)] * len(whole_before),
            out_specs=pl.BlockSpec(memory_space=pl.ANY),
            input_output_aliases={count: 0} if whole_before else {},
            scratch_shapes=[pltpu.VMEM((ranks, size, lanes), F32), pltpu.SemaphoreType.DMA],
            compiler_params=PARAMS,
            cost_estimate=COST if step < len(spans) - 1 else None,
            name="add_ranks",
        )(core, *parts, *whole_before)
        begin += size
    return out


AXES = ("gx", "gy", "gz")


def exchange(x, sizes, **bits):
    order = [(gx, gy, gz) for gx in range(sizes["gx"]) for gy in range(sizes["gy"]) for gz in range(sizes["gz"])]
    place = {index: at for at, index in enumerate(order)}
    moves = [bits.get(axis, 0) for axis in AXES]
    pairs = [(at, place[tuple(i ^ move for i, move in zip(index, moves))]) for at, index in enumerate(order)]
    return lax.ppermute(x, AXES, pairs)


def steps_of(size):
    return [1 << b for b in range(size.bit_length() - 1)]


def body(sizes, field, test):
    second = field.shape[1]
    early, raw, last = second * 4 // 32, second * 6 // 32, second * 8 // 32
    sketch, pairs, first_field = partial_sketch(field, test, early)
    for bit in steps_of(sizes["gz"]):
        sketch = sketch + exchange(sketch, sizes, gz=bit | 1)
        if bit == 1:
            first_field = run(copy_kernel, "first_field", first_field, sketch, first_field)
    for bit in steps_of(sizes["gy"]):
        sketch = sketch + exchange(sketch, sizes, gy=bit, gz=1)
    return project(sketch, pairs, first_field, sizes, raw, (second - early - raw - last, last))


def solution(mesh):
    in_specs = (P("gx", "gy", "gz"), P(None, "gy", "gz"))
    out_specs = P("gx", "gy", "gz")
    step = functools.partial(body, dict(mesh.shape))
    return jax.shard_map(step, mesh=mesh, in_specs=in_specs, out_specs=out_specs, check_vma=False)
```

```python
import functools

import jax
import jax.numpy as jnp
from jax import lax
from jax.experimental import pallas as pl
from jax.experimental.pallas import tpu as pltpu
from jax.sharding import PartitionSpec as P

F32, BF16 = jnp.float32, jnp.bfloat16
PRECISE = lax.Precision.HIGHEST
NT = (((1,), (1,)), ((), ()))
NN = (((1,), (0,)), ((), ()))
LANES, SUBLANES = 128, 8
VMEM_LIMIT = 48 << 20


def split(x, parts):
    terms = []
    for _ in range(parts - 1):
        terms.append(x.astype(BF16))
        x = x - terms[-1].astype(F32)
    return terms + [x.astype(BF16)]


def sketch_kernel(span, field_hbm, test_hbm, sketch_ref, pairs_ref, first_ref, field, test, sems):
    rows, second, lanes = field_hbm.shape
    columns = test_hbm.shape[0]
    steps = second // span
    copies = []
    for step in range(steps):
        part = pl.ds(step * span, span)
        for which, (source, target) in enumerate(((field_hbm, field), (test_hbm, test))):
            copy = pltpu.make_async_copy(source.at[:, part], target.at[step], sems.at[which, step])
            copy.start()
            copies.append(copy)
    total = low = None
    for step in range(steps):
        copies[2 * step].wait()
        copies[2 * step + 1].wait()
        flat_field = field.at[step].reshape(rows * span, lanes)
        flat_test = test.at[step].reshape(columns * span, lanes)
        for pair in range(span // 2):
            x = [flat_field[pl.ds(2 * pair + q, rows, stride=span), :] for q in range(2)]
            for q in range(2):
                if step * span + 2 * pair + q < first_ref.shape[0]:
                    first_ref[step * span + 2 * pair + q] = x[q]
            x = jnp.concatenate(x, axis=1)
            t = jnp.concatenate([flat_test[pl.ds(2 * pair + q, columns, stride=span), :] for q in range(2)], axis=1)
            x = split(x, 3)
            t = split(t, 3)
            weights = jnp.concatenate(x[:2], axis=0)
            pairs_ref[step * span // 2 + pair] = weights
            term = lax.dot_general(jnp.concatenate(t, axis=0), weights, NT, preferred_element_type=F32)
            rest = lax.dot_general(t[0], x[2], NT, preferred_element_type=F32)
            total = term if total is None else total + term
            low = rest if low is None else low + rest
    for part in reversed(range(3)):
        block = total[part * columns : (part + 1) * columns]
        low = low + block[:, rows:] + block[:, :rows] if part else (low + block[:, rows:]) + block[:, :rows]
    sketch_ref[...] = low


def partial_sketch(field, test, first):
    rows, second, lanes = field.shape
    columns = test.shape[0]
    span = SUBLANES
    steps = second // span
    return pl.pallas_call(
        functools.partial(sketch_kernel, span),
        in_specs=[pl.BlockSpec(memory_space=pl.ANY)] * 2,
        out_shape=[
            jax.ShapeDtypeStruct((columns, rows), F32),
            jax.ShapeDtypeStruct((second // 2, 2 * rows, 2 * lanes), BF16),
            jax.ShapeDtypeStruct((first, rows, lanes), F32),
        ],
        scratch_shapes=[
            pltpu.VMEM((steps, rows, span, lanes), F32),
            pltpu.VMEM((steps, columns, span, lanes), F32),
            pltpu.SemaphoreType.DMA((2, steps)),
        ],
        compiler_params=pltpu.CompilerParams(vmem_limit_bytes=VMEM_LIMIT),
        name="partial_sketch",
    )(*(pltpu.with_memory_space_constraint(array, pltpu.HBM) for array in (field, test)))


def unit(size):
    return jnp.where(
        lax.broadcasted_iota(jnp.int32, (size, size), 0) == lax.broadcasted_iota(jnp.int32, (size, size), 1), 1.0, 0.0
    ).astype(F32)


def eliminate(gram, right, spread_ref):
    size, width = gram.shape[0], LANES + right.shape[1]
    whole = jnp.concatenate([unit(size), gram, jnp.zeros((size, LANES - 2 * size), F32), right], axis=1)
    tiles = [whole[i : i + SUBLANES] for i in range(0, size, SUBLANES)]
    spread = lambda x: jnp.broadcast_to(x, (SUBLANES, LANES))
    widen = lambda x: jnp.concatenate([x] * (width // LANES), axis=1)
    block = range(SUBLANES)
    solved = []
    for t, tile in enumerate(tiles):
        start = size + t * SUBLANES
        for j in block:
            spread_ref[t, j] = spread(tile[:, start + j : start + j + 1])
        entry = {(i, j): spread(spread_ref[t, j, i : i + 1, :]) for j in block for i in range(j, SUBLANES)}
        inverse, lower = [], {}
        for j in block:
            inverse.append(1.0 / entry[j, j])
            for i in range(j + 1, SUBLANES):
                lower[i, j] = entry[i, j] * inverse[j]
            for m in range(j + 1, SUBLANES):
                for i in range(m, SUBLANES):
                    entry[i, m] = entry[i, m] - lower[i, j] * entry[m, j]
        lower = {at: widen(x) for at, x in lower.items()}
        reduced = []
        for i in block:
            row = jnp.broadcast_to(tile[i : i + 1], (SUBLANES, width))
            for j in range(i):
                row = row - lower[i, j] * reduced[j]
            reduced.append(row)
            solved.append((row * widen(lax.rsqrt(entry[i, i])))[:1])
        if t == len(tiles) - 1:
            break
        scaled = [None] * SUBLANES
        for i in reversed(block):
            row = reduced[i] * widen(inverse[i])
            for j in range(i + 1, SUBLANES):
                row = row - lower[j, i] * scaled[j]
            scaled[i] = row
        for later in range(t + 1, len(tiles)):
            rest = tiles[later]
            for j in block:
                rest = rest - tiles[later][:, start + j : start + j + 1] * scaled[j]
            tiles[later] = rest
    return jnp.concatenate(solved, axis=0)


def twice(factor):
    high, low = (part.astype(F32) for part in split(factor, 2))
    left = jnp.concatenate([high, low], axis=0)
    return jnp.concatenate([left, left], axis=1).astype(BF16)


def times(left, pair):
    product = lax.dot_general(left, pair, NN, preferred_element_type=F32)
    half = left.shape[0] // 2
    return product[:half] + product[half:]


def multiply(factor, pairs_ref, first, out_refs, begin=0):
    span, ranks, lanes = out_refs[0].shape
    left = twice(factor)
    for pair in range((span - begin) // 2):
        product = times(left, pairs_ref[first + pair])
        for q in range(2):
            for d, ref in enumerate(out_refs):
                ref[begin + 2 * pair + q] = product[d * ranks : (d + 1) * ranks, q * lanes : (q + 1) * lanes]


def copy_kernel(sketch_ref, field_ref, out_ref):
    out_ref[...] = field_ref[...]


def mark_kernel(sketch_ref, out_ref):
    out_ref[...] = sketch_ref[...]


def raw_kernel(first, sketch_ref, pairs_ref, out_ref):
    multiply(sketch_ref[...], pairs_ref, first, [out_ref])


def solve_kernel(axis, first, sketch_ref, pairs_ref, solved_ref, *refs):
    *out_refs, spread_ref = refs
    rows = pairs_ref.shape[1] // 2
    sketch = sketch_ref[...]
    gram = lax.dot_general(sketch, sketch, NT, precision=PRECISE, preferred_element_type=F32)
    solved = eliminate(gram, sketch[:, :rows], spread_ref)
    parties = len(out_refs) + 1
    ranks = solved.shape[0] // parties
    me = lax.axis_index(axis)
    ordered = []
    for d in range(parties):
        rank_rows = solved[:ranks]
        for e in range(1, parties):
            rank_rows = jnp.where((me ^ d) == e, solved[e * ranks : (e + 1) * ranks], rank_rows)
        ordered.append(rank_rows)
    solved_ref[...] = jnp.concatenate(ordered, axis=0)
    multiply(jnp.concatenate(ordered[1:], axis=0)[:, LANES:], pairs_ref, first, out_refs)


def others_kernel(first, solved_ref, pairs_ref, *out_refs):
    ranks = out_refs[0].shape[1]
    multiply(solved_ref[ranks : ranks * (1 + len(out_refs)), LANES:], pairs_ref, first, out_refs)


def own_kernel(parties, whole_pairs, raw_pairs, sketch_ref, solved_ref, pairs_ref, *refs):
    *refs, out_ref = refs
    field_refs, raw_refs = refs[: parties - 1], refs[parties - 1 :]
    span, ranks, lanes = out_ref.shape
    columns, rows = sketch_ref.shape[0], sketch_ref.shape[1] // parties
    solved = solved_ref[:ranks, :]
    inverse = solved[:, :columns]
    apply = functools.partial(lax.dot_general, dimension_numbers=NN, precision=PRECISE, preferred_element_type=F32)
    done = whole_pairs + raw_pairs
    multiply(solved[:, LANES:], pairs_ref, done, [out_ref], 2 * done)
    lefts = [twice(solved[:, LANES:])]
    lefts += [twice(apply(inverse, sketch_ref[:, d * rows : (d + 1) * rows])) for d in range(1, parties)]
    for pair in range(done):
        if pair < whole_pairs:
            product = times(lefts[0], pairs_ref[pair])
            for left, ref in zip(lefts[1:], field_refs):
                terms = split(jnp.concatenate([ref[2 * pair], ref[2 * pair + 1]], axis=1), 2)
                product = product + times(left, jnp.concatenate(terms, axis=0))
        else:
            right = []
            for at in (2 * (pair - whole_pairs), 2 * (pair - whole_pairs) + 1):
                total = raw_refs[0][at]
                for ref in raw_refs[1:]:
                    total = total + ref[at]
                right.append(total)
            product = apply(inverse, jnp.concatenate(right, axis=1))
        for q in range(2):
            out_ref[2 * pair + q] = product[:, q * lanes : (q + 1) * lanes]


def add_kernel(parties, begin, size, own_ref, *refs):
    *others, out_hbm, total_ref, sem = refs
    others = others[: parties - 1]
    ranks, span, lanes = total_ref.shape
    flat = total_ref.reshape(ranks * span, lanes)
    bare = size - others[0].shape[0]
    for at in range(size):
        total = own_ref[begin + at]
        for part in others if at >= bare else ():
            total = total + part[at - bare]
        flat[pl.ds(at, ranks, stride=span), :] = total
    copy = pltpu.make_async_copy(total_ref, out_hbm.at[:, pl.ds(begin, size)], sem)
    copy.start()
    copy.wait()


PARAMS = pltpu.CompilerParams(vmem_limit_bytes=VMEM_LIMIT)
COST = pl.CostEstimate(flops=1 << 30, bytes_accessed=1 << 25, transcendentals=0)


def run(kernel, name, out_shape, *operands, cost=COST, scratch=()):
    if isinstance(out_shape, jax.Array):
        out_shape = jax.ShapeDtypeStruct(out_shape.shape, out_shape.dtype)
    return pl.pallas_call(
        kernel, out_shape=out_shape, compiler_params=PARAMS, cost_estimate=cost, name=name, scratch_shapes=scratch
    )(*operands)


def project(sketch, pairs, first_field, sizes, raw, spans):
    parties = sizes["gx"]
    columns, rows = sketch.shape[0], pairs.shape[1] // 2
    lanes = pairs.shape[2] // 2
    ranks, second = columns // parties, 2 * pairs.shape[0]
    piece = lambda span, height: jax.ShapeDtypeStruct((span, height, lanes), F32)
    early = first_field.shape[0]
    fields = [exchange(first_field, sizes, gx=d) for d in range(1, parties)]
    whole = sketch
    summed = whole
    for bit in steps_of(parties):
        whole = jnp.concatenate([whole, exchange(whole, sizes, gx=bit)], axis=1)
    mine = run(functools.partial(raw_kernel, early // 2), "raw_product", piece(raw, columns), summed, pairs, cost=RAW_COST)
    raw_parts = [mine] + [exchange(mine, sizes, gx=d) for d in range(1, parties)]
    whole, *fields = lax.optimization_barrier([whole, *fields])
    place, received = early + raw, []
    solved, *sent = run(
        functools.partial(solve_kernel, "gx", place // 2),
        "solve",
        [jax.ShapeDtypeStruct((columns, LANES + rows), F32)] + [piece(spans[0], ranks)] * (parties - 1),
        whole,
        pairs,
        scratch=[pltpu.VMEM((columns // SUBLANES, SUBLANES, SUBLANES, LANES), F32)],
    )
    for step, span in enumerate(spans):
        if step:
            sent = run(
                functools.partial(others_kernel, place // 2),
                "others_ranks",
                [piece(span, ranks)] * (parties - 1),
                solved,
                pairs,
            )
        received += [exchange(x, sizes, gx=d + 1) for d, x in enumerate(sent)]
        place += span
    core = run(
        functools.partial(own_kernel, parties, early // 2, raw // 2),
        "own_ranks",
        piece(second, ranks),
        whole,
        solved,
        pairs,
        *fields,
        *raw_parts,
    )
    out, begin = None, 0
    for step, span in enumerate(spans):
        size = span if step else early + raw + span
        whole_before = [] if out is None else [out]
        count = 1 + (parties - 1)
        parts = received[step * (parties - 1) : (step + 1) * (parties - 1)]
        out = pl.pallas_call(
            functools.partial(add_kernel, parties, begin, size),
            out_shape=jax.ShapeDtypeStruct((ranks, second, lanes), F32),
            in_specs=[pl.BlockSpec(memory_space=pltpu.VMEM)] * count + [pl.BlockSpec(memory_space=pl.ANY)] * len(whole_before),
            out_specs=pl.BlockSpec(memory_space=pl.ANY),
            input_output_aliases={count: 0} if whole_before else {},
            scratch_shapes=[pltpu.VMEM((ranks, size, lanes), F32), pltpu.SemaphoreType.DMA],
            compiler_params=PARAMS,
            cost_estimate=COST if step < len(spans) - 1 else None,
            name="add_ranks",
        )(core, *parts, *whole_before)
        begin += size
    return out


HELD_COST = pl.CostEstimate(flops=1 << 30, bytes_accessed=8 << 20, transcendentals=0)
RAW_COST = pl.CostEstimate(flops=1 << 30, bytes_accessed=32 << 20, transcendentals=0)
AXES = ("gx", "gy", "gz")


def exchange(x, sizes, **bits):
    order = [(gx, gy, gz) for gx in range(sizes["gx"]) for gy in range(sizes["gy"]) for gz in range(sizes["gz"])]
    place = {index: at for at, index in enumerate(order)}
    moves = [bits.get(axis, 0) for axis in AXES]
    pairs = [(at, place[tuple(i ^ move for i, move in zip(index, moves))]) for at, index in enumerate(order)]
    return lax.ppermute(x, AXES, pairs)


def steps_of(size):
    return [1 << b for b in range(size.bit_length() - 1)]


def body(sizes, field, test):
    second = field.shape[1]
    early, raw, last = second * 6 // 32, second * 6 // 32, second * 8 // 32
    sketch, pairs, first_field = partial_sketch(field, test, early)
    for bit in steps_of(sizes["gz"]):
        sketch = sketch + exchange(sketch, sizes, gz=bit | 1)
        if bit == 1:
            first_field = run(copy_kernel, "first_field", first_field, sketch, first_field)
    for bit in steps_of(sizes["gy"]):
        coming = exchange(sketch, sizes, gy=bit, gz=1)
        if bit:
            sketch = run(mark_kernel, "held", jax.ShapeDtypeStruct(sketch.shape, F32), sketch, cost=HELD_COST)
        sketch = sketch + coming
    return project(sketch, pairs, first_field, sizes, raw, (second - early - raw - last, last))


def solution(mesh):
    in_specs = (P("gx", "gy", "gz"), P(None, "gy", "gz"))
    out_specs = P("gx", "gy", "gz")
    step = functools.partial(body, dict(mesh.shape))
    return jax.shard_map(step, mesh=mesh, in_specs=in_specs, out_specs=out_specs, check_vma=False)
```

```python
import functools

import jax
import jax.numpy as jnp
from jax import lax
from jax.experimental import pallas as pl
from jax.experimental.pallas import tpu as pltpu
from jax.sharding import PartitionSpec as P

F32, BF16 = jnp.float32, jnp.bfloat16
PRECISE = lax.Precision.HIGHEST
NT = (((1,), (1,)), ((), ()))
NN = (((1,), (0,)), ((), ()))
LANES, SUBLANES = 128, 8
VMEM_LIMIT = 48 << 20


def split(x, parts):
    terms = []
    for _ in range(parts - 1):
        terms.append(x.astype(BF16))
        x = x - terms[-1].astype(F32)
    return terms + [x.astype(BF16)]


def sketch_kernel(span, field_hbm, test_hbm, sketch_ref, pairs_ref, first_ref, field, test, sems):
    rows, second, lanes = field_hbm.shape
    columns = test_hbm.shape[0]
    steps = second // span
    copies = []
    for step in range(steps):
        part = pl.ds(step * span, span)
        for which, (source, target) in enumerate(((field_hbm, field), (test_hbm, test))):
            copy = pltpu.make_async_copy(source.at[:, part], target.at[step], sems.at[which, step])
            copy.start()
            copies.append(copy)
    total = low = None
    dot = functools.partial(lax.dot_general, dimension_numbers=NN, preferred_element_type=F32)
    for step in range(steps):
        copies[2 * step].wait()
        copies[2 * step + 1].wait()
        flat_field = field.at[step].reshape(rows * span, lanes)
        flat_test = test.at[step].reshape(columns * span, lanes)
        for pair in range(span // 2):
            x = [flat_field[pl.ds(2 * pair + q, rows, stride=span), :] for q in range(2)]
            t = [flat_test[pl.ds(2 * pair + q, columns, stride=span), :] for q in range(2)]
            for q in range(2):
                if step * span + 2 * pair + q < first_ref.shape[0]:
                    first_ref[step * span + 2 * pair + q] = x[q]
            pairs_ref[step * span // 2 + pair] = jnp.concatenate(split(jnp.concatenate(x, axis=1), 2), axis=0)
            t = split(jnp.concatenate(t, axis=1), 3)
            turned = split(jnp.concatenate([part.T for part in x], axis=0), 3)
            term = dot(jnp.concatenate(t, axis=0), jnp.concatenate(turned[:2], axis=1))
            rest = dot(t[0], turned[2])
            total = term if total is None else total + term
            low = rest if low is None else low + rest
    for part in reversed(range(3)):
        block = total[part * columns : (part + 1) * columns]
        low = (low + block[:, rows:]) + block[:, :rows]
    sketch_ref[...] = low


def partial_sketch(field, test, first):
    rows, second, lanes = field.shape
    columns = test.shape[0]
    span = SUBLANES
    steps = second // span
    return pl.pallas_call(
        functools.partial(sketch_kernel, span),
        in_specs=[pl.BlockSpec(memory_space=pl.ANY)] * 2,
        out_shape=[
            jax.ShapeDtypeStruct((columns, rows), F32),
            jax.ShapeDtypeStruct((second // 2, 2 * rows, 2 * lanes), BF16),
            jax.ShapeDtypeStruct((first, rows, lanes), F32),
        ],
        scratch_shapes=[
            pltpu.VMEM((steps, rows, span, lanes), F32),
            pltpu.VMEM((steps, columns, span, lanes), F32),
            pltpu.SemaphoreType.DMA((2, steps)),
        ],
        compiler_params=pltpu.CompilerParams(vmem_limit_bytes=VMEM_LIMIT),
        name="partial_sketch",
    )(*(pltpu.with_memory_space_constraint(array, pltpu.HBM) for array in (field, test)))


def unit(size):
    return jnp.where(
        lax.broadcasted_iota(jnp.int32, (size, size), 0) == lax.broadcasted_iota(jnp.int32, (size, size), 1), 1.0, 0.0
    ).astype(F32)


def eliminate(gram, right, spread_ref):
    size, width = gram.shape[0], LANES + right.shape[1]
    whole = jnp.concatenate([unit(size), gram, jnp.zeros((size, LANES - 2 * size), F32), right], axis=1)
    tiles = [whole[i : i + SUBLANES] for i in range(0, size, SUBLANES)]
    spread = lambda x: jnp.broadcast_to(x, (SUBLANES, LANES))
    widen = lambda x: jnp.concatenate([x] * (width // LANES), axis=1)
    block = range(SUBLANES)
    solved = []
    for t, tile in enumerate(tiles):
        start = size + t * SUBLANES
        for j in block:
            spread_ref[t, j] = spread(tile[:, start + j : start + j + 1])
        entry = {(i, j): spread(spread_ref[t, j, i : i + 1, :]) for j in block for i in range(j, SUBLANES)}
        inverse, lower = [], {}
        for j in block:
            inverse.append(1.0 / entry[j, j])
            for i in range(j + 1, SUBLANES):
                lower[i, j] = entry[i, j] * inverse[j]
            for m in range(j + 1, SUBLANES):
                for i in range(m, SUBLANES):
                    entry[i, m] = entry[i, m] - lower[i, j] * entry[m, j]
        lower = {at: widen(x) for at, x in lower.items()}
        reduced = []
        for i in block:
            row = jnp.broadcast_to(tile[i : i + 1], (SUBLANES, width))
            for j in range(i):
                row = row - lower[i, j] * reduced[j]
            reduced.append(row)
            solved.append((row * widen(lax.rsqrt(entry[i, i])))[:1])
        if t == len(tiles) - 1:
            break
        scaled = [None] * SUBLANES
        for i in reversed(block):
            row = reduced[i] * widen(inverse[i])
            for j in range(i + 1, SUBLANES):
                row = row - lower[j, i] * scaled[j]
            scaled[i] = row
        for later in range(t + 1, len(tiles)):
            rest = tiles[later]
            for j in block:
                rest = rest - tiles[later][:, start + j : start + j + 1] * scaled[j]
            tiles[later] = rest
    return jnp.concatenate(solved, axis=0)


def twice(factor):
    high, low = (part.astype(F32) for part in split(factor, 2))
    left = jnp.concatenate([high, low], axis=0)
    return jnp.concatenate([left, left], axis=1).astype(BF16)


def times(left, pair):
    product = lax.dot_general(left, pair, NN, preferred_element_type=F32)
    half = left.shape[0] // 2
    return product[:half] + product[half:]


def multiply(factor, pairs_ref, first, out_refs, begin=0):
    span, ranks, lanes = out_refs[0].shape
    left = twice(factor)
    for pair in range((span - begin) // 2):
        product = times(left, pairs_ref[first + pair])
        for q in range(2):
            for d, ref in enumerate(out_refs):
                ref[begin + 2 * pair + q] = product[d * ranks : (d + 1) * ranks, q * lanes : (q + 1) * lanes]


def copy_kernel(sketch_ref, field_ref, out_ref):
    out_ref[...] = field_ref[...]


def mark_kernel(sketch_ref, out_ref):
    out_ref[...] = sketch_ref[...]


def raw_kernel(first, sketch_ref, pairs_ref, out_ref):
    multiply(sketch_ref[...], pairs_ref, first, [out_ref])


def solve_kernel(axis, first, sketch_ref, pairs_ref, solved_ref, *refs):
    *out_refs, spread_ref = refs
    rows = pairs_ref.shape[1] // 2
    sketch = sketch_ref[...]
    gram = lax.dot_general(sketch, sketch, NT, precision=PRECISE, preferred_element_type=F32)
    solved = eliminate(gram, sketch[:, :rows], spread_ref)
    parties = len(out_refs) + 1
    ranks = solved.shape[0] // parties
    me = lax.axis_index(axis)
    ordered = []
    for d in range(parties):
        rank_rows = solved[:ranks]
        for e in range(1, parties):
            rank_rows = jnp.where((me ^ d) == e, solved[e * ranks : (e + 1) * ranks], rank_rows)
        ordered.append(rank_rows)
    solved_ref[...] = jnp.concatenate(ordered, axis=0)
    multiply(jnp.concatenate(ordered[1:], axis=0)[:, LANES:], pairs_ref, first, out_refs)


def others_kernel(first, solved_ref, pairs_ref, *out_refs):
    ranks = out_refs[0].shape[1]
    multiply(solved_ref[ranks : ranks * (1 + len(out_refs)), LANES:], pairs_ref, first, out_refs)


def own_kernel(parties, whole_pairs, raw_pairs, sketch_ref, solved_ref, pairs_ref, *refs):
    *refs, out_ref = refs
    field_refs, raw_refs = refs[: parties - 1], refs[parties - 1 :]
    span, ranks, lanes = out_ref.shape
    columns, rows = sketch_ref.shape[0], sketch_ref.shape[1] // parties
    solved = solved_ref[:ranks, :]
    inverse = solved[:, :columns]
    apply = functools.partial(lax.dot_general, dimension_numbers=NN, precision=PRECISE, preferred_element_type=F32)
    done = whole_pairs + raw_pairs
    multiply(solved[:, LANES:], pairs_ref, done, [out_ref], 2 * done)
    lefts = [twice(solved[:, LANES:])]
    lefts += [twice(apply(inverse, sketch_ref[:, d * rows : (d + 1) * rows])) for d in range(1, parties)]
    for pair in range(done):
        if pair < whole_pairs:
            product = times(lefts[0], pairs_ref[pair])
            for left, ref in zip(lefts[1:], field_refs):
                terms = split(jnp.concatenate([ref[2 * pair], ref[2 * pair + 1]], axis=1), 2)
                product = product + times(left, jnp.concatenate(terms, axis=0))
        else:
            right = []
            for at in (2 * (pair - whole_pairs), 2 * (pair - whole_pairs) + 1):
                total = raw_refs[0][at]
                for ref in raw_refs[1:]:
                    total = total + ref[at]
                right.append(total)
            product = apply(inverse, jnp.concatenate(right, axis=1))
        for q in range(2):
            out_ref[2 * pair + q] = product[:, q * lanes : (q + 1) * lanes]


def add_kernel(parties, begin, size, own_ref, *refs):
    *others, out_hbm, total_ref, sem = refs
    others = others[: parties - 1]
    ranks, span, lanes = total_ref.shape
    flat = total_ref.reshape(ranks * span, lanes)
    bare = size - others[0].shape[0]
    for at in range(size):
        total = own_ref[begin + at]
        for part in others if at >= bare else ():
            total = total + part[at - bare]
        flat[pl.ds(at, ranks, stride=span), :] = total
    copy = pltpu.make_async_copy(total_ref, out_hbm.at[:, pl.ds(begin, size)], sem)
    copy.start()
    copy.wait()


PARAMS = pltpu.CompilerParams(vmem_limit_bytes=VMEM_LIMIT)
COST = pl.CostEstimate(flops=1 << 30, bytes_accessed=1 << 25, transcendentals=0)


def run(kernel, name, out_shape, *operands, cost=COST, scratch=()):
    if isinstance(out_shape, jax.Array):
        out_shape = jax.ShapeDtypeStruct(out_shape.shape, out_shape.dtype)
    return pl.pallas_call(
        kernel, out_shape=out_shape, compiler_params=PARAMS, cost_estimate=cost, name=name, scratch_shapes=scratch
    )(*operands)


def project(sketch, pairs, first_field, sizes, raw, spans):
    parties = sizes["gx"]
    columns, rows = sketch.shape[0], pairs.shape[1] // 2
    lanes = pairs.shape[2] // 2
    ranks, second = columns // parties, 2 * pairs.shape[0]
    piece = lambda span, height: jax.ShapeDtypeStruct((span, height, lanes), F32)
    early = first_field.shape[0]
    fields = [exchange(first_field, sizes, gx=d) for d in range(1, parties)]
    whole = sketch
    summed = whole
    for bit in steps_of(parties):
        whole = jnp.concatenate([whole, exchange(whole, sizes, gx=bit)], axis=1)
    mine = run(functools.partial(raw_kernel, early // 2), "raw_product", piece(raw, columns), summed, pairs, cost=RAW_COST)
    raw_parts = [mine] + [exchange(mine, sizes, gx=d) for d in range(1, parties)]
    whole, *fields = lax.optimization_barrier([whole, *fields])
    place, received = early + raw, []
    solved, *sent = run(
        functools.partial(solve_kernel, "gx", place // 2),
        "solve",
        [jax.ShapeDtypeStruct((columns, LANES + rows), F32)] + [piece(spans[0], ranks)] * (parties - 1),
        whole,
        pairs,
        scratch=[pltpu.VMEM((columns // SUBLANES, SUBLANES, SUBLANES, LANES), F32)],
    )
    for step, span in enumerate(spans):
        if step:
            sent = run(
                functools.partial(others_kernel, place // 2),
                "others_ranks",
                [piece(span, ranks)] * (parties - 1),
                solved,
                pairs,
            )
        received += [exchange(x, sizes, gx=d + 1) for d, x in enumerate(sent)]
        place += span
    core = run(
        functools.partial(own_kernel, parties, early // 2, raw // 2),
        "own_ranks",
        piece(second, ranks),
        whole,
        solved,
        pairs,
        *fields,
        *raw_parts,
    )
    out, begin = None, 0
    for step, span in enumerate(spans):
        size = span if step else early + raw + span
        whole_before = [] if out is None else [out]
        count = 1 + (parties - 1)
        parts = received[step * (parties - 1) : (step + 1) * (parties - 1)]
        out = pl.pallas_call(
            functools.partial(add_kernel, parties, begin, size),
            out_shape=jax.ShapeDtypeStruct((ranks, second, lanes), F32),
            in_specs=[pl.BlockSpec(memory_space=pltpu.VMEM)] * count + [pl.BlockSpec(memory_space=pl.ANY)] * len(whole_before),
            out_specs=pl.BlockSpec(memory_space=pl.ANY),
            input_output_aliases={count: 0} if whole_before else {},
            scratch_shapes=[pltpu.VMEM((ranks, size, lanes), F32), pltpu.SemaphoreType.DMA],
            compiler_params=PARAMS,
            cost_estimate=COST if step < len(spans) - 1 else None,
            name="add_ranks",
        )(core, *parts, *whole_before)
        begin += size
    return out


HELD_COST = pl.CostEstimate(flops=1 << 30, bytes_accessed=8 << 20, transcendentals=0)
RAW_COST = pl.CostEstimate(flops=1 << 30, bytes_accessed=32 << 20, transcendentals=0)
AXES = ("gx", "gy", "gz")


def exchange(x, sizes, **bits):
    order = [(gx, gy, gz) for gx in range(sizes["gx"]) for gy in range(sizes["gy"]) for gz in range(sizes["gz"])]
    place = {index: at for at, index in enumerate(order)}
    moves = [bits.get(axis, 0) for axis in AXES]
    pairs = [(at, place[tuple(i ^ move for i, move in zip(index, moves))]) for at, index in enumerate(order)]
    return lax.ppermute(x, AXES, pairs)


def steps_of(size):
    return [1 << b for b in range(size.bit_length() - 1)]


def body(sizes, field, test):
    second = field.shape[1]
    early, raw, last = second * 6 // 32, second * 6 // 32, second * 8 // 32
    sketch, pairs, first_field = partial_sketch(field, test, early)
    for bit in steps_of(sizes["gz"]):
        sketch = sketch + exchange(sketch, sizes, gz=bit | 1)
        if bit == 1:
            first_field = run(copy_kernel, "first_field", first_field, sketch, first_field)
    for bit in steps_of(sizes["gy"]):
        coming = exchange(sketch, sizes, gy=bit, gz=1)
        if bit:
            sketch = run(mark_kernel, "held", jax.ShapeDtypeStruct(sketch.shape, F32), sketch, cost=HELD_COST)
        sketch = sketch + coming
    return project(sketch, pairs, first_field, sizes, raw, (second - early - raw - last, last))


def solution(mesh):
    in_specs = (P("gx", "gy", "gz"), P(None, "gy", "gz"))
    out_specs = P("gx", "gy", "gz")
    step = functools.partial(body, dict(mesh.shape))
    return jax.shard_map(step, mesh=mesh, in_specs=in_specs, out_specs=out_specs, check_vma=False)
```

```python
import functools

import jax
import jax.numpy as jnp
from jax import lax
from jax.experimental import pallas as pl
from jax.experimental.pallas import tpu as pltpu
from jax.sharding import PartitionSpec as P

F32, BF16 = jnp.float32, jnp.bfloat16
PRECISE = lax.Precision.HIGHEST
NT = (((1,), (1,)), ((), ()))
NN = (((1,), (0,)), ((), ()))
LANES, SUBLANES = 128, 8
VMEM_LIMIT = 48 << 20


def split(x, parts):
    terms = []
    for _ in range(parts - 1):
        terms.append(x.astype(BF16))
        x = x - terms[-1].astype(F32)
    return terms + [x.astype(BF16)]


def sketch_kernel(span, field_hbm, test_hbm, sketch_ref, pairs_ref, first_ref, field, test, sems):
    rows, second, lanes = field_hbm.shape
    columns = test_hbm.shape[0]
    steps = second // span
    copies = []
    for step in range(steps):
        part = pl.ds(step * span, span)
        for which, (source, target) in enumerate(((field_hbm, field), (test_hbm, test))):
            copy = pltpu.make_async_copy(
                source.at[:, part], target.at[step, pl.ds(0, source.shape[0])], sems.at[which, step]
            )
            copy.start()
            copies.append(copy)
    total = low = None
    dot = functools.partial(lax.dot_general, dimension_numbers=NN, preferred_element_type=F32)
    for step in range(steps):
        copies[2 * step].wait()
        copies[2 * step + 1].wait()
        flat_field = field.at[step].reshape((rows + 1) * span, lanes)
        flat_test = test.at[step].reshape((columns + 1) * span, lanes)
        for pair in range(span // 2):
            x = [flat_field[pl.ds(2 * pair + q, rows, stride=span), :] for q in range(2)]
            t = [flat_test[pl.ds(2 * pair + q, columns, stride=span), :] for q in range(2)]
            for q in range(2):
                if step * span + 2 * pair + q < first_ref.shape[0]:
                    first_ref[step * span + 2 * pair + q] = x[q]
            pairs_ref[step * span // 2 + pair] = jnp.concatenate(split(jnp.concatenate(x, axis=1), 2), axis=0)
            t = split(jnp.concatenate(t, axis=1), 3)
            turned = split(jnp.concatenate([part.T for part in x], axis=0), 3)
            term = dot(jnp.concatenate(t, axis=0), jnp.concatenate(turned[:2], axis=1))
            rest = dot(t[0], turned[2])
            total = term if total is None else total + term
            low = rest if low is None else low + rest
    for part in reversed(range(3)):
        block = total[part * columns : (part + 1) * columns]
        low = (low + block[:, rows:]) + block[:, :rows]
    sketch_ref[...] = low


def partial_sketch(field, test, first):
    rows, second, lanes = field.shape
    columns = test.shape[0]
    span = SUBLANES
    steps = second // span
    return pl.pallas_call(
        functools.partial(sketch_kernel, span),
        in_specs=[pl.BlockSpec(memory_space=pl.ANY)] * 2,
        out_shape=[
            jax.ShapeDtypeStruct((columns, rows), F32),
            jax.ShapeDtypeStruct((second // 2, 2 * rows, 2 * lanes), BF16),
            jax.ShapeDtypeStruct((first, rows, lanes), F32),
        ],
        scratch_shapes=[
            pltpu.VMEM((steps, rows + 1, span, lanes), F32),
            pltpu.VMEM((steps, columns + 1, span, lanes), F32),
            pltpu.SemaphoreType.DMA((2, steps)),
        ],
        compiler_params=pltpu.CompilerParams(vmem_limit_bytes=VMEM_LIMIT),
        name="partial_sketch",
    )(*(pltpu.with_memory_space_constraint(array, pltpu.HBM) for array in (field, test)))


def unit(size):
    return jnp.where(
        lax.broadcasted_iota(jnp.int32, (size, size), 0) == lax.broadcasted_iota(jnp.int32, (size, size), 1), 1.0, 0.0
    ).astype(F32)


def eliminate(gram, right, spread_ref):
    size, width = gram.shape[0], LANES + right.shape[1]
    whole = jnp.concatenate([unit(size), gram, jnp.zeros((size, LANES - 2 * size), F32), right], axis=1)
    tiles = [whole[i : i + SUBLANES] for i in range(0, size, SUBLANES)]
    spread = lambda x: jnp.broadcast_to(x, (SUBLANES, LANES))
    widen = lambda x: jnp.concatenate([x] * (width // LANES), axis=1)
    block = range(SUBLANES)
    solved = []
    for t, tile in enumerate(tiles):
        start = size + t * SUBLANES
        for j in block:
            spread_ref[t, j] = spread(tile[:, start + j : start + j + 1])
        entry = {(i, j): spread(spread_ref[t, j, i : i + 1, :]) for j in block for i in range(j, SUBLANES)}
        inverse, lower = [], {}
        for j in block:
            inverse.append(1.0 / entry[j, j])
            for i in range(j + 1, SUBLANES):
                lower[i, j] = entry[i, j] * inverse[j]
            for m in range(j + 1, SUBLANES):
                for i in range(m, SUBLANES):
                    entry[i, m] = entry[i, m] - lower[i, j] * entry[m, j]
        lower = {at: widen(x) for at, x in lower.items()}
        reduced = []
        for i in block:
            row = jnp.broadcast_to(tile[i : i + 1], (SUBLANES, width))
            for j in range(i):
                row = row - lower[i, j] * reduced[j]
            reduced.append(row)
            solved.append((row * widen(lax.rsqrt(entry[i, i])))[:1])
        if t == len(tiles) - 1:
            break
        scaled = [None] * SUBLANES
        for i in reversed(block):
            row = reduced[i] * widen(inverse[i])
            for j in range(i + 1, SUBLANES):
                row = row - lower[j, i] * scaled[j]
            scaled[i] = row
        for later in range(t + 1, len(tiles)):
            rest = tiles[later]
            for j in block:
                rest = rest - tiles[later][:, start + j : start + j + 1] * scaled[j]
            tiles[later] = rest
    return jnp.concatenate(solved, axis=0)


def twice(factor):
    high, low = (part.astype(F32) for part in split(factor, 2))
    left = jnp.concatenate([high, low], axis=0)
    return jnp.concatenate([left, left], axis=1).astype(BF16)


def times(left, pair):
    product = lax.dot_general(left, pair, NN, preferred_element_type=F32)
    half = left.shape[0] // 2
    return product[:half] + product[half:]


def multiply(factor, pairs_ref, first, out_refs, begin=0):
    span, ranks, lanes = out_refs[0].shape
    left = twice(factor)
    for pair in range((span - begin) // 2):
        product = times(left, pairs_ref[first + pair])
        for q in range(2):
            for d, ref in enumerate(out_refs):
                ref[begin + 2 * pair + q] = product[d * ranks : (d + 1) * ranks, q * lanes : (q + 1) * lanes]


def copy_kernel(sketch_ref, field_ref, out_ref):
    out_ref[...] = field_ref[...]


def mark_kernel(sketch_ref, out_ref):
    out_ref[...] = sketch_ref[...]


def raw_kernel(first, sketch_ref, pairs_ref, out_ref):
    multiply(sketch_ref[...], pairs_ref, first, [out_ref])


def solve_kernel(axis, first, sketch_ref, pairs_ref, solved_ref, *refs):
    *out_refs, spread_ref = refs
    rows = pairs_ref.shape[1] // 2
    sketch = sketch_ref[...]
    gram = lax.dot_general(sketch, sketch, NT, precision=PRECISE, preferred_element_type=F32)
    solved = eliminate(gram, sketch[:, :rows], spread_ref)
    parties = len(out_refs) + 1
    ranks = solved.shape[0] // parties
    me = lax.axis_index(axis)
    ordered = []
    for d in range(parties):
        rank_rows = solved[:ranks]
        for e in range(1, parties):
            rank_rows = jnp.where((me ^ d) == e, solved[e * ranks : (e + 1) * ranks], rank_rows)
        ordered.append(rank_rows)
    solved_ref[...] = jnp.concatenate(ordered, axis=0)
    multiply(jnp.concatenate(ordered[1:], axis=0)[:, LANES:], pairs_ref, first, out_refs)


def others_kernel(first, solved_ref, pairs_ref, *out_refs):
    ranks = out_refs[0].shape[1]
    multiply(solved_ref[ranks : ranks * (1 + len(out_refs)), LANES:], pairs_ref, first, out_refs)


def own_kernel(parties, whole_pairs, raw_pairs, sketch_ref, solved_ref, pairs_ref, *refs):
    *refs, out_ref = refs
    field_refs, raw_refs = refs[: parties - 1], refs[parties - 1 :]
    span, ranks, lanes = out_ref.shape
    columns, rows = sketch_ref.shape[0], sketch_ref.shape[1] // parties
    solved = solved_ref[:ranks, :]
    inverse = solved[:, :columns]
    apply = functools.partial(lax.dot_general, dimension_numbers=NN, precision=PRECISE, preferred_element_type=F32)
    done = whole_pairs + raw_pairs
    multiply(solved[:, LANES:], pairs_ref, done, [out_ref], 2 * done)
    lefts = [twice(solved[:, LANES:])]
    lefts += [twice(apply(inverse, sketch_ref[:, d * rows : (d + 1) * rows])) for d in range(1, parties)]
    for pair in range(done):
        if pair < whole_pairs:
            product = times(lefts[0], pairs_ref[pair])
            for left, ref in zip(lefts[1:], field_refs):
                terms = split(jnp.concatenate([ref[2 * pair], ref[2 * pair + 1]], axis=1), 2)
                product = product + times(left, jnp.concatenate(terms, axis=0))
        else:
            right = []
            for at in (2 * (pair - whole_pairs), 2 * (pair - whole_pairs) + 1):
                total = raw_refs[0][at]
                for ref in raw_refs[1:]:
                    total = total + ref[at]
                right.append(total)
            product = apply(inverse, jnp.concatenate(right, axis=1))
        for q in range(2):
            out_ref[2 * pair + q] = product[:, q * lanes : (q + 1) * lanes]


def add_kernel(parties, begin, size, own_ref, *refs):
    *others, out_hbm, total_ref, sem = refs
    others = others[: parties - 1]
    ranks, span, lanes = out_hbm.shape[0], *total_ref.shape[1:]
    flat = total_ref.reshape((ranks + 1) * span, lanes)
    bare = size - others[0].shape[0]
    for at in range(size):
        total = own_ref[begin + at]
        for part in others if at >= bare else ():
            total = total + part[at - bare]
        flat[pl.ds(at, ranks, stride=span), :] = total
    copy = pltpu.make_async_copy(total_ref.at[pl.ds(0, ranks)], out_hbm.at[:, pl.ds(begin, size)], sem)
    copy.start()
    copy.wait()


PARAMS = pltpu.CompilerParams(vmem_limit_bytes=VMEM_LIMIT)
COST = pl.CostEstimate(flops=1 << 30, bytes_accessed=1 << 25, transcendentals=0)


def run(kernel, name, out_shape, *operands, cost=COST, scratch=()):
    if isinstance(out_shape, jax.Array):
        out_shape = jax.ShapeDtypeStruct(out_shape.shape, out_shape.dtype)
    return pl.pallas_call(
        kernel, out_shape=out_shape, compiler_params=PARAMS, cost_estimate=cost, name=name, scratch_shapes=scratch
    )(*operands)


def project(sketch, pairs, first_field, sizes, raw, spans):
    parties = sizes["gx"]
    columns, rows = sketch.shape[0], pairs.shape[1] // 2
    lanes = pairs.shape[2] // 2
    ranks, second = columns // parties, 2 * pairs.shape[0]
    piece = lambda span, height: jax.ShapeDtypeStruct((span, height, lanes), F32)
    early = first_field.shape[0]
    fields = [exchange(first_field, sizes, gx=d) for d in range(1, parties)]
    whole = sketch
    summed = whole
    for bit in steps_of(parties):
        whole = jnp.concatenate([whole, exchange(whole, sizes, gx=bit)], axis=1)
    mine = run(functools.partial(raw_kernel, early // 2), "raw_product", piece(raw, columns), summed, pairs, cost=RAW_COST)
    raw_parts = [mine] + [exchange(mine, sizes, gx=d) for d in range(1, parties)]
    whole, *fields = lax.optimization_barrier([whole, *fields])
    place, received = early + raw, []
    solved, *sent = run(
        functools.partial(solve_kernel, "gx", place // 2),
        "solve",
        [jax.ShapeDtypeStruct((columns, LANES + rows), F32)] + [piece(spans[0], ranks)] * (parties - 1),
        whole,
        pairs,
        scratch=[pltpu.VMEM((columns // SUBLANES, SUBLANES, SUBLANES, LANES), F32)],
    )
    for step, span in enumerate(spans):
        if step:
            sent = run(
                functools.partial(others_kernel, place // 2),
                "others_ranks",
                [piece(span, ranks)] * (parties - 1),
                solved,
                pairs,
            )
        received += [exchange(x, sizes, gx=d + 1) for d, x in enumerate(sent)]
        place += span
    core = run(
        functools.partial(own_kernel, parties, early // 2, raw // 2),
        "own_ranks",
        piece(second, ranks),
        whole,
        solved,
        pairs,
        *fields,
        *raw_parts,
    )
    out, begin = None, 0
    for step, span in enumerate(spans):
        size = span if step else early + raw + span
        whole_before = [] if out is None else [out]
        count = 1 + (parties - 1)
        parts = received[step * (parties - 1) : (step + 1) * (parties - 1)]
        out = pl.pallas_call(
            functools.partial(add_kernel, parties, begin, size),
            out_shape=jax.ShapeDtypeStruct((ranks, second, lanes), F32),
            in_specs=[pl.BlockSpec(memory_space=pltpu.VMEM)] * count + [pl.BlockSpec(memory_space=pl.ANY)] * len(whole_before),
            out_specs=pl.BlockSpec(memory_space=pl.ANY),
            input_output_aliases={count: 0} if whole_before else {},
            scratch_shapes=[pltpu.VMEM((ranks + 1, size, lanes), F32), pltpu.SemaphoreType.DMA],
            compiler_params=PARAMS,
            cost_estimate=COST if step < len(spans) - 1 else None,
            name="add_ranks",
        )(core, *parts, *whole_before)
        begin += size
    return out


HELD_COST = pl.CostEstimate(flops=1 << 30, bytes_accessed=8 << 20, transcendentals=0)
RAW_COST = pl.CostEstimate(flops=1 << 30, bytes_accessed=32 << 20, transcendentals=0)
AXES = ("gx", "gy", "gz")


def exchange(x, sizes, **bits):
    order = [(gx, gy, gz) for gx in range(sizes["gx"]) for gy in range(sizes["gy"]) for gz in range(sizes["gz"])]
    place = {index: at for at, index in enumerate(order)}
    moves = [bits.get(axis, 0) for axis in AXES]
    pairs = [(at, place[tuple(i ^ move for i, move in zip(index, moves))]) for at, index in enumerate(order)]
    return lax.ppermute(x, AXES, pairs)


def steps_of(size):
    return [1 << b for b in range(size.bit_length() - 1)]


def body(sizes, field, test):
    second = field.shape[1]
    early, raw, last = second * 6 // 32, second * 6 // 32, second * 8 // 32
    sketch, pairs, first_field = partial_sketch(field, test, early)
    for bit in steps_of(sizes["gz"]):
        sketch = sketch + exchange(sketch, sizes, gz=bit | 1)
        if bit == 1:
            first_field = run(copy_kernel, "first_field", first_field, sketch, first_field)
    for bit in steps_of(sizes["gy"]):
        coming = exchange(sketch, sizes, gy=bit, gz=1)
        if bit:
            sketch = run(mark_kernel, "held", jax.ShapeDtypeStruct(sketch.shape, F32), sketch, cost=HELD_COST)
        sketch = sketch + coming
    return project(sketch, pairs, first_field, sizes, raw, (second - early - raw - last, last))


def solution(mesh):
    in_specs = (P("gx", "gy", "gz"), P(None, "gy", "gz"))
    out_specs = P("gx", "gy", "gz")
    step = functools.partial(body, dict(mesh.shape))
    return jax.shard_map(step, mesh=mesh, in_specs=in_specs, out_specs=out_specs, check_vma=False)
```
